32 devices in a mesh: blk: 4 (over y, x), band: 8 (over z, core).
Axes of the slice: x: 2, y: 2, z: 4, core: 2. Of those that a mesh axis runs over, the one named last changes fastest.
Arguments:
- fine_blocks: float32 [128, 64, 256], P(('blk', 'band')), may hold values from -3 to 3
- source_group: int32 [128, 4], P(('blk', 'band')), may hold values from 0 to 3, all different within a row; in each aligned block of 4 rows (0 to 3, 4 to 7, ...) at most 4 rows name the same one
- source_row: int32 [128, 4], P(('blk', 'band')), may hold values from 0 to 3
- prolong_blocks: float32 [128, 64, 128], P(('blk', 'band')), may hold values from -0.75 to 0.75
- prolong_code: int32 [128, 2], P(('blk', 'band')), may hold values from 0 to 2
Outputs:
- coarse_rows: float32 [2048, 1280], P(('blk', 'band'))
The draws below stay inside these ranges and needn't reach their ends.
Inputs may be any that keep to these rules, and one draw needn't show every extreme that they name: `source_group`: each fine block row names 4 different groups; among the rows of one device no group is named more than 4 times, and some device names one group exactly 4 times.
All inputs are finite; a program needn't handle non-finite values.
Results may differ from the reference program's by a relative error of at most 0.0003.
Values sent between devices are 32-bit elements; how exact they have to be, the bound alone decides.
No kernel may reach another device: no remote copies, remote signals or barrier semaphores. Data moves between devices by JAX's collectives and lax.ppermute only.
A program may use at most 64 MiB of HBM per device.

```python
import math
import jax
import jax.numpy as jnp
import numpy as np
from jax import lax

B = 64
FB = 4
KA = 4
KP = 2
CB = 1
MB = 4
NF = 128
N_BLK = 4
N_BAND = 8


def place_ends(values, key, smallest, largest):
    index_at = [jax.random.randint(jax.random.fold_in(key, axis), (), 0, length) for axis, length in enumerate(values.shape)]
    widest = values.shape.index(max(values.shape))
    neighbour = index_at[:widest] + [(index_at[widest] + 1) % values.shape[widest]] + index_at[widest + 1:]
    return values.at[tuple(index_at)].set(smallest).at[tuple(neighbour)].set(largest)


def level_of(key, extent, pieces, smallest, largest):
    factor_of, own = 1.0, jax.random.fold_in(key, 6)
    for axis_at, parts in pieces:
        steps = jnp.exp(jax.random.uniform(jax.random.fold_in(own, axis_at), (parts,), jnp.float32, smallest / len(pieces), largest / len(pieces)))
        factor_of = factor_of * jnp.repeat(steps, extent[axis_at] // parts).reshape([-1 if axis == axis_at else 1 for axis in range(len(extent))])
    return factor_of


def routed_block(rng, own, number, rows, count, top, bound, lean):
    sequence = jax.random.permutation(rng, count)
    crowded, usual = portions_of(count, rows * top, bound, lean, True), portions_of(count, rows * top, bound, lean, False)
    places = jnp.arange(count)

    def named(tallies, turn):
        used = int((tallies > 0).sum())
        fixed = max(1, used // 4)
        shifted = fixed + (places - fixed + turn * (used - fixed)) % max(1, count - fixed)
        return jnp.zeros((count,), jnp.int32).at[sequence[jnp.where(places < fixed, places, shifted)]].set(jnp.asarray(tallies, jnp.int32))

    tallies = jnp.where(number % 4 == 0, named(crowded, number // 4), named(usual, number - number // 4 - 1))
    mixed = jax.random.permutation(jax.random.fold_in(own, 3), count)
    giver, taker = mixed[0:count // 2 * 2:2], mixed[1:count // 2 * 2:2]
    margin = jnp.minimum(tallies[giver] - 1, bound - tallies[taker]) // 2
    margin = jnp.where((giver == sequence[0]) | (taker == sequence[0]) | (tallies[taker] == 0), 0, jnp.maximum(margin, 0))
    shifted = jax.random.randint(jax.random.fold_in(own, 4), (count // 2,), 0, 1 << 20) % (margin + 1)
    tallies = tallies.at[giver].add(-shifted).at[taker].add(shifted)
    members = jnp.searchsorted(jnp.cumsum(tallies), jnp.arange(rows * top), side="right").astype(jnp.int32)
    table = members.reshape(top, rows).T
    table = table[jax.random.permutation(jax.random.fold_in(own, 1), rows)]
    turn = jax.random.randint(jax.random.fold_in(own, 2), (rows, 1), 0, top)
    return jnp.take_along_axis(table, (jnp.arange(top)[None, :] + turn) % top, axis=1)


def portions_of(number_of, total, most, skew, full):
    portions = [(1 << 20) // math.isqrt(rank ** skew) + 1 for rank in range(1, number_of + 1)]
    largest = most if full else min(most, max(-(-total // number_of), total * portions[0] // sum(portions)))
    least = 1 if total - largest >= number_of - 1 else 0
    given, spare = [largest] + [least] * (number_of - 1), total - largest - least * (number_of - 1)
    while spare > 0:
        free = [i for i in range(1, number_of) if given[i] < largest] or [i for i in range(1, number_of) if given[i] < most]
        whole, left = sum([portions[i] for i in free]), spare
        for i in free:
            more = min(most - given[i], max(1, left * portions[i] // whole), spare)
            given[i] = given[i] + more
            spare = spare - more
    return np.array(given)


def noise(own_key, dims, deviation, reach, pieces=(), kind=jnp.bfloat16):
    entries = jax.random.normal(own_key, dims, jnp.float32) * deviation
    if len(pieces) > 0:
        entries = level_of(own_key, dims, pieces, -0.22, 0.18) * entries
    return jnp.clip(entries, min=-reach, max=reach).astype(kind)


def setup_inputs(seed: int = 0) -> dict:
    keys = jax.random.split(jax.random.key(seed), 6)
    fine_blocks = noise(keys[0], (NF, B, KA * B), 0.5, 3.0, ((0, 32),), jnp.float32)
    source_group_keys = jax.random.split(jax.random.fold_in(keys[1], 1), NF // FB)
    source_group_turns = jax.random.permutation(jax.random.fold_in(keys[1], 3), NF // FB)
    source_group = jax.vmap(lambda own, number: routed_block(jax.random.fold_in(keys[1], 2), own, number, FB, N_BLK, KA, MB, 2))(source_group_keys, source_group_turns).reshape((NF, KA))
    source_row = place_ends(jax.random.randint(keys[2], (NF, KA), 0, FB), jax.random.fold_in(keys[2], 1), 0, FB - 1).astype(jnp.int32)
    prolong_blocks = noise(keys[3], (NF, B, KP * B), B ** -0.5, 0.75, ((0, 32),), jnp.float32)
    prolong_code = place_ends(jax.random.randint(keys[4], (NF, KP), 0, 3 * CB), jax.random.fold_in(keys[4], 1), 0, (3 * CB) - 1).astype(jnp.int32)
    return {"fine_blocks": fine_blocks, "source_group": source_group, "source_row": source_row, "prolong_blocks": prolong_blocks, "prolong_code": prolong_code}


def reference(fine_blocks, source_group, source_row, prolong_blocks, prolong_code):
    devices_all = N_BLK * N_BAND
    fine_total = FB * devices_all
    window_blocks = 5 * N_BLK * CB
    a_tiles = fine_blocks.reshape(fine_total, B, KA, B).transpose(0, 2, 1, 3)
    p_tiles = prolong_blocks.reshape(fine_total, B, KP, B)
    coarse = jnp.zeros((CB * devices_all, B, window_blocks, B), jnp.float32)

    def one_device(coarse, device):
        group_id = device // N_BAND
        band_id = device % N_BAND
        first_row = device * FB
        a_here = lax.dynamic_slice_in_dim(a_tiles, first_row, FB, 0)
        p_here = lax.dynamic_slice_in_dim(p_tiles, first_row, FB, 0)
        code_here = lax.dynamic_slice_in_dim(prolong_code, first_row, FB, 0)
        group_here = lax.dynamic_slice_in_dim(source_group, first_row, FB, 0)
        row_here = lax.dynamic_slice_in_dim(source_row, first_row, FB, 0)
        source = (group_here * N_BAND + band_id) * FB + row_here
        p_source = p_tiles[source]
        code_source = prolong_code[source]
        left_part = jnp.einsum("ianx,ikab->inkxb", p_here, a_here, precision=lax.Precision.HIGHEST)
        products = jnp.einsum("inkxb,ikbmy->inkmxy", left_part, p_source, precision=lax.Precision.HIGHEST)
        shift_n = code_here // CB
        slot_n = code_here % CB
        shift_m = code_source // CB
        slot_m = code_source % CB
        owner_device = group_id * N_BAND + (band_id + shift_n - 1) % N_BAND
        row_block = owner_device * CB + slot_n
        offset = shift_m[:, None, :, :] - shift_n[:, :, None, None] + 2
        col_block = (offset * N_BLK + group_here[:, None, :, None]) * CB + slot_m[:, None, :, :]
        row_all = jnp.broadcast_to(row_block[:, :, None, None], col_block.shape)
        coarse = coarse.at[row_all.reshape(-1), :, col_block.reshape(-1), :].add(products.reshape(-1, B, B))
        return coarse, None

    coarse, unused_out = lax.scan(one_device, coarse, jnp.arange(devices_all, dtype=jnp.int32))
    return coarse.reshape(CB * devices_all * B, window_blocks * B)
```

```python
import functools

import jax
import jax.numpy as jnp
from jax import lax
from jax.experimental import pallas as pl
from jax.experimental.pallas import tpu as pltpu
from jax.sharding import PartitionSpec as P

SHIFTS = 3


def vmem():
    return pl.BlockSpec(memory_space=pltpu.VMEM)


def smem():
    return pl.BlockSpec(memory_space=pltpu.SMEM)


def split(x):
    hi = x.astype(jnp.bfloat16)
    return hi, (x - hi.astype(jnp.float32)).astype(jnp.bfloat16)


def dot(a, b):
    return lax.dot_general(a, b, (((1,), (0,)), ((), ())), preferred_element_type=jnp.float32)


def dot3(a_hi, a_lo, b_hi, b_lo):
    return dot(a_hi, b_hi) + (dot(a_hi, b_lo) + dot(a_lo, b_hi))


def pack_kernel(width, code_ref, p_ref, out_ref):
    rows = p_ref.shape[0]
    for i in range(rows):
        out_ref[i * width : (i + 1) * width, :] = p_ref[i]
    lane = lax.broadcasted_iota(jnp.int32, (1, 2 * width), 1)
    left = lane < width
    masks = []
    for i in range(rows):
        c0, c1 = code_ref[i, 0], code_ref[i, 1]
        straight = jnp.where(left, c0, c1)
        crossed = jnp.where(left, c1, c0)
        near = jnp.where(left, 0, 1)
        far = jnp.where(left, 2, -1)
        masks += [straight == near, crossed == near, straight == far, crossed == far]
    out_ref[rows * width :, :] = jnp.concatenate([m.astype(jnp.float32) for m in masks], axis=0)


def left_kernel(width, groups, group_ref, code_ref, a_ref, p_ref, hi_ref, lo_ref):
    rows, per_row = group_ref.shape
    me = lax.axis_index("blk")
    odd = lax.axis_index("band") % 2
    pair = 2 * width
    wide = rows * width
    pt = p_ref[...].reshape(wide, pair).T
    row_of = lax.broadcasted_iota(jnp.int32, (1, wide), 1) // width
    codes = []
    for n in range(2):
        c = jnp.full((1, wide), code_ref[0, n], jnp.int32)
        for i in range(1, rows):
            c = jnp.where(row_of == i, code_ref[i, n], c)
        codes.append(c)
    blocks = []
    for dest in (1, 2 - 2 * odd, 2 * odd):
        blocks.append(
            jnp.where(codes[0] == dest, pt[:width], 0.0) + jnp.where(codes[1] == dest, pt[width:], 0.0)
        )
    rt_hi, rt_lo = split(jnp.concatenate(blocks, axis=0))
    half = lax.broadcasted_iota(jnp.int32, (width, pair), 1) // width
    for p in range(rows // 2):
        tops = []
        for h in range(2):
            i = 2 * p + h
            cells = []
            for k in range(per_row):
                x = a_ref[i, :, (k // 2) * pair : (k // 2 + 1) * pair]
                if k % 2 != h:
                    x = pltpu.roll(x, width, 1)
                cells.append(jnp.where(half == h, x, 0.0))
            tops.append(cells)
        lanes = slice(p * pair, (p + 1) * pair)
        for j in range(groups):
            g = me ^ j
            parts = []
            for h in range(2):
                x = jnp.zeros((width, pair), jnp.float32)
                for k in range(per_row):
                    x = jnp.where(group_ref[2 * p + h, k] == g, tops[h][k], x)
                parts.append(x)
            b_hi, b_lo = split(jnp.concatenate(parts, axis=0))
            left = dot3(rt_hi[:, lanes], rt_lo[:, lanes], b_hi, b_lo)
            l_hi, l_lo = split(left)
            hi_ref[j, :, lanes] = l_hi
            lo_ref[j, :, lanes] = l_lo


def right_kernel(width, groups, group_ref, row_ref, hi_ref, lo_ref, *refs):
    sources, (own_ref, chip_ref, far_ref) = refs[:groups], refs[groups:]
    rows, per_row = group_ref.shape
    me = lax.axis_index("blk")
    pair = 2 * width
    right_half = lax.broadcasted_iota(jnp.int32, (width, pair), 1) >= width
    for q in range(groups // 2):
        found = []
        for j in (2 * q, 2 * q + 1):
            g = me ^ j
            src = sources[j]
            near, far = [], []
            for i in range(rows):
                s = jnp.int32(0)
                for k in range(per_row):
                    s = jnp.where(group_ref[i, k] == g, row_ref[i, k], s)
                x = src[pl.ds(pl.multiple_of(s * width, width), width), :]
                y = pltpu.roll(x, width, 1)
                m = [src[pl.ds(rows * width + 4 * s + t, 1), :] for t in range(4)]
                near.append(x * m[0] + y * m[1])
                far.append(x * m[2] + y * m[3])
            w = jnp.concatenate([jnp.concatenate(near, axis=0), jnp.concatenate(far, axis=0)], axis=1)
            w_hi, w_lo = split(w)
            found.append(dot3(hi_ref[j], lo_ref[j], w_hi, w_lo))
        swap = me % 2 == 1
        base = ((me ^ (2 * q)) // 2) * pair
        for t, out_ref in enumerate((own_ref, chip_ref, far_ref)):
            a, b = (f[t * width : (t + 1) * width] for f in found)
            first = jnp.where(swap, b, a)
            second = jnp.where(swap, a, b)
            for e in range(SHIFTS):
                tile = slice((e // 2) * pair, (e // 2 + 1) * pair)
                u, v = first[:, tile], second[:, tile]
                if e % 2 == 0:
                    v = pltpu.roll(v, width, 1)
                else:
                    u = pltpu.roll(u, width, 1)
                place = pl.multiple_of(e * groups * width + base, pair)
                out_ref[:, pl.ds(place, pair)] = jnp.where(right_half, v, u)


def add_kernel(step, own_ref, chip_ref, far_ref, out_ref):
    odd = lax.axis_index("band") % 2 == 1
    upper = lambda t: jnp.where(odd, far_ref[:, t], chip_ref[:, t])
    lower = lambda t: jnp.where(odd, chip_ref[:, t], far_ref[:, t])
    at = [slice(e * step, (e + 1) * step) for e in range(5)]
    out_ref[:, at[0]] = lower(at[0])
    out_ref[:, at[1]] = lower(at[1]) + own_ref[:, at[0]]
    out_ref[:, at[2]] = lower(at[2]) + own_ref[:, at[1]] + upper(at[0])
    out_ref[:, at[3]] = own_ref[:, at[2]] + upper(at[1])
    out_ref[:, at[4]] = upper(at[2])


def body(fine_blocks, source_group, source_row, prolong_blocks, prolong_code):
    rows, width, pair = prolong_blocks.shape
    groups = lax.axis_size("blk")
    bands = lax.axis_size("band")
    f32 = jnp.float32
    packed_rows = rows * width + 4 * rows
    packed = pl.pallas_call(
        functools.partial(pack_kernel, width),
        out_shape=jax.ShapeDtypeStruct((packed_rows, pair), f32),
        in_specs=[smem(), vmem()],
        out_specs=vmem(),
        name="pack",
    )(prolong_code, prolong_blocks)
    arrived = [packed] + [
        lax.ppermute(packed, "blk", [(i, i ^ j) for i in range(groups)]) for j in range(1, groups)
    ]
    height = SHIFTS * width
    deep = rows * width
    hi, lo = pl.pallas_call(
        functools.partial(left_kernel, width, groups),
        out_shape=[jax.ShapeDtypeStruct((groups, height, deep), jnp.bfloat16)] * 2,
        in_specs=[smem(), smem(), vmem(), vmem()],
        out_specs=[vmem()] * 2,
        cost_estimate=pl.CostEstimate(flops=2 * 3 * groups * height * 128 * deep, bytes_accessed=2000000, transcendentals=0),
        name="left",
    )(source_group, prolong_code, fine_blocks, prolong_blocks)
    own, chip, far = pl.pallas_call(
        functools.partial(right_kernel, width, groups),
        out_shape=[jax.ShapeDtypeStruct((width, SHIFTS * groups * width), f32)] * 3,
        in_specs=[smem()] * 2 + [vmem()] * (2 + groups),
        out_specs=[vmem()] * 3,
        name="right",
    )(source_group, source_row, hi, lo, *arrived)
    chip = lax.ppermute(chip, "band", [(i, i ^ 1) for i in range(bands)])
    far = lax.ppermute(far, "band", [(i, (i + 1 if i % 2 else i - 1) % bands) for i in range(bands)])
    return pl.pallas_call(
        functools.partial(add_kernel, groups * width),
        out_shape=jax.ShapeDtypeStruct((width, 5 * groups * width), f32),
        in_specs=[vmem()] * 3,
        out_specs=vmem(),
        name="add",
    )(own, chip, far)


def solution(mesh):
    return jax.shard_map(
        body,
        mesh=mesh,
        in_specs=(
            P(("blk", "band"), None, None),
            P(("blk", "band"), None),
            P(("blk", "band"), None),
            P(("blk", "band"), None, None),
            P(("blk", "band"), None),
        ),
        out_specs=P(("blk", "band"), None),
        check_vma=False,
    )
```

```python
import functools

import jax
import jax.numpy as jnp
from jax import lax
from jax.experimental import pallas as pl
from jax.experimental.pallas import tpu as pltpu
from jax.sharding import PartitionSpec as P

SHIFTS = 3
PARAMS = pltpu.CompilerParams(vmem_limit_bytes=24 * 1024 * 1024)


def vmem():
    return pl.BlockSpec(memory_space=pltpu.VMEM)


def smem():
    return pl.BlockSpec(memory_space=pltpu.SMEM)


def split(x):
    hi = x.astype(jnp.bfloat16)
    return hi, (x - hi.astype(jnp.float32)).astype(jnp.bfloat16)


def dot(a, b):
    return lax.dot_general(a, b, (((1,), (0,)), ((), ())), preferred_element_type=jnp.float32)


def dot3(a_hi, a_lo, b_hi, b_lo):
    return dot(a_hi, b_hi) + (dot(a_hi, b_lo) + dot(a_lo, b_hi))


def pack_kernel(width, code_ref, p_ref, out_ref):
    rows = p_ref.shape[0]
    for i in range(rows):
        out_ref[i * width : (i + 1) * width, :] = p_ref[i]
    lane = lax.broadcasted_iota(jnp.int32, (1, 2 * width), 1)
    left = lane < width
    masks = []
    for i in range(rows):
        c0, c1 = code_ref[0, i], code_ref[1, i]
        straight = jnp.where(left, c0, c1)
        crossed = jnp.where(left, c1, c0)
        near = jnp.where(left, 0, 1)
        far = jnp.where(left, 2, -1)
        masks += [straight == near, crossed == near, straight == far, crossed == far]
    out_ref[rows * width :, :] = jnp.concatenate([m.astype(jnp.float32) for m in masks], axis=0)


def left_kernel(width, groups, group_ref, code_ref, a_ref, p_ref, hi_ref, lo_ref):
    rows, per_row = group_ref.shape
    me = lax.axis_index("blk")
    odd = lax.axis_index("band") % 2
    pair = 2 * width
    wide = rows * width
    pt = p_ref[...].reshape(wide, pair).T
    row_of = lax.broadcasted_iota(jnp.int32, (1, wide), 1) // width
    codes = []
    for n in range(2):
        c = jnp.full((1, wide), code_ref[n, 0], jnp.int32)
        for i in range(1, rows):
            c = jnp.where(row_of == i, code_ref[n, i], c)
        codes.append(c)
    blocks = []
    for dest in (1, 2 - 2 * odd, 2 * odd):
        blocks.append(
            jnp.where(codes[0] == dest, pt[:width], 0.0) + jnp.where(codes[1] == dest, pt[width:], 0.0)
        )
    rt_hi, rt_lo = split(jnp.concatenate(blocks, axis=0))
    half = lax.broadcasted_iota(jnp.int32, (width, pair), 1) // width
    for p in range(rows // 2):
        tops = []
        for h in range(2):
            i = 2 * p + h
            cells = []
            for k in range(per_row):
                x = a_ref[i, :, (k // 2) * pair : (k // 2 + 1) * pair]
                if k % 2 != h:
                    x = pltpu.roll(x, width, 1)
                cells.append(jnp.where(half == h, x, 0.0))
            tops.append(cells)
        lanes = slice(p * pair, (p + 1) * pair)
        for j in range(groups):
            g = me ^ j
            parts = []
            for h in range(2):
                x = jnp.zeros((width, pair), jnp.float32)
                for k in range(per_row):
                    x = jnp.where(group_ref[2 * p + h, k] == g, tops[h][k], x)
                parts.append(x)
            b_hi, b_lo = split(jnp.concatenate(parts, axis=0))
            left = dot3(rt_hi[:, lanes], rt_lo[:, lanes], b_hi, b_lo)
            l_hi, l_lo = split(left)
            hi_ref[j, :, lanes] = l_hi
            lo_ref[j, :, lanes] = l_lo


def right_kernel(width, groups, group_ref, row_ref, hi_ref, lo_ref, *refs):
    sources, (own_ref, chip_ref, far_ref) = refs[:groups], refs[groups:]
    rows, per_row = group_ref.shape
    me = lax.axis_index("blk")
    pair = 2 * width
    right_half = lax.broadcasted_iota(jnp.int32, (width, pair), 1) >= width
    for q in range(groups // 2):
        found = []
        for j in (2 * q, 2 * q + 1):
            g = me ^ j
            src = sources[j]
            near, far = [], []
            for i in range(rows):
                s = jnp.int32(0)
                for k in range(per_row):
                    s = jnp.where(group_ref[i, k] == g, row_ref[i, k], s)
                x = src[pl.ds(pl.multiple_of(s * width, width), width), :]
                y = pltpu.roll(x, width, 1)
                m = [src[pl.ds(rows * width + 4 * s + t, 1), :] for t in range(4)]
                near.append(x * m[0] + y * m[1])
                far.append(x * m[2] + y * m[3])
            w = jnp.concatenate([jnp.concatenate(near, axis=0), jnp.concatenate(far, axis=0)], axis=1)
            w_hi, w_lo = split(w)
            found.append(dot3(hi_ref[j], lo_ref[j], w_hi, w_lo))
        swap = me % 2 == 1
        base = ((me ^ (2 * q)) // 2) * pair
        for t, out_ref in enumerate((own_ref, chip_ref, far_ref)):
            a, b = (f[t * width : (t + 1) * width] for f in found)
            first = jnp.where(swap, b, a)
            second = jnp.where(swap, a, b)
            for e in range(SHIFTS):
                tile = slice((e // 2) * pair, (e // 2 + 1) * pair)
                u, v = first[:, tile], second[:, tile]
                if e % 2 == 0:
                    v = pltpu.roll(v, width, 1)
                else:
                    u = pltpu.roll(u, width, 1)
                place = pl.multiple_of(e * groups * width + base, pair)
                out_ref[:, pl.ds(place, pair)] = jnp.where(right_half, v, u)


def add_kernel(step, own_ref, chip_ref, far_ref, out_ref):
    odd = lax.axis_index("band") % 2 == 1
    upper = lambda t: jnp.where(odd, far_ref[:, t], chip_ref[:, t])
    lower = lambda t: jnp.where(odd, chip_ref[:, t], far_ref[:, t])
    at = [slice(e * step, (e + 1) * step) for e in range(5)]
    out_ref[:, at[0]] = lower(at[0])
    out_ref[:, at[1]] = lower(at[1]) + own_ref[:, at[0]]
    out_ref[:, at[2]] = lower(at[2]) + own_ref[:, at[1]] + upper(at[0])
    out_ref[:, at[3]] = own_ref[:, at[2]] + upper(at[1])
    out_ref[:, at[4]] = upper(at[2])


def body(fine_blocks, source_group, source_row, prolong_blocks, prolong_code):
    rows, width, pair = prolong_blocks.shape
    groups = lax.axis_size("blk")
    bands = lax.axis_size("band")
    f32 = jnp.float32
    prolong_code = prolong_code.T
    packed_rows = rows * width + 4 * rows
    packed = pl.pallas_call(
        functools.partial(pack_kernel, width),
        out_shape=jax.ShapeDtypeStruct((packed_rows, pair), f32),
        in_specs=[smem(), vmem()],
        out_specs=vmem(),
        compiler_params=PARAMS,
        name="pack",
    )(prolong_code, prolong_blocks)
    arrived = [packed] + [
        lax.ppermute(packed, "blk", [(i, i ^ j) for i in range(groups)]) for j in range(1, groups)
    ]
    height = SHIFTS * width
    deep = rows * width
    hi, lo = pl.pallas_call(
        functools.partial(left_kernel, width, groups),
        out_shape=[jax.ShapeDtypeStruct((groups, height, deep), jnp.bfloat16)] * 2,
        in_specs=[smem(), smem(), vmem(), vmem()],
        out_specs=[vmem()] * 2,
        cost_estimate=pl.CostEstimate(flops=2 * 3 * groups * height * 128 * deep, bytes_accessed=2000000, transcendentals=0),
        compiler_params=PARAMS,
        name="left",
    )(source_group, prolong_code, fine_blocks, prolong_blocks)
    own, chip, far = pl.pallas_call(
        functools.partial(right_kernel, width, groups),
        out_shape=[jax.ShapeDtypeStruct((width, SHIFTS * groups * width), f32)] * 3,
        in_specs=[smem()] * 2 + [vmem()] * (2 + groups),
        out_specs=[vmem()] * 3,
        compiler_params=PARAMS,
        name="right",
    )(source_group, source_row, hi, lo, *arrived)
    chip = lax.ppermute(chip, "band", [(i, i ^ 1) for i in range(bands)])
    far = lax.ppermute(far, "band", [(i, (i + 1 if i % 2 else i - 1) % bands) for i in range(bands)])
    return pl.pallas_call(
        functools.partial(add_kernel, groups * width),
        out_shape=jax.ShapeDtypeStruct((width, 5 * groups * width), f32),
        in_specs=[vmem()] * 3,
        out_specs=vmem(),
        compiler_params=PARAMS,
        name="add",
    )(own, chip, far)


def solution(mesh):
    return jax.shard_map(
        body,
        mesh=mesh,
        in_specs=(
            P(("blk", "band"), None, None),
            P(("blk", "band"), None),
            P(("blk", "band"), None),
            P(("blk", "band"), None, None),
            P(("blk", "band"), None),
        ),
        out_specs=P(("blk", "band"), None),
        check_vma=False,
    )
```

```python
import functools

import jax
import jax.numpy as jnp
from jax import lax
from jax.experimental import pallas as pl
from jax.experimental.pallas import tpu as pltpu
from jax.sharding import PartitionSpec as P

SHIFTS = 3
CHUNKS = 2
PARAMS = pltpu.CompilerParams(vmem_limit_bytes=24 * 1024 * 1024)


def vmem():
    return pl.BlockSpec(memory_space=pltpu.VMEM)


def smem():
    return pl.BlockSpec(memory_space=pltpu.SMEM)


def split(x):
    hi = x.astype(jnp.bfloat16)
    return hi, (x - hi.astype(jnp.float32)).astype(jnp.bfloat16)


def dot(a, b):
    return lax.dot_general(a, b, (((1,), (0,)), ((), ())), preferred_element_type=jnp.float32)


def dot3(a_hi, a_lo, b_hi, b_lo):
    return dot(a_hi, b_hi) + (dot(a_hi, b_lo) + dot(a_lo, b_hi))


def pack_kernel(width, code_hbm, p_hbm, out_ref, code_ref, sems):
    rows = code_ref.shape[1]
    codes = pltpu.make_async_copy(code_hbm, code_ref, sems.at[0])
    blocks = pltpu.make_async_copy(p_hbm, out_ref.at[0 : rows * width], sems.at[1])
    codes.start()
    blocks.start()
    codes.wait()
    lane = lax.broadcasted_iota(jnp.int32, (1, 2 * width), 1)
    left = lane < width
    masks = []
    for i in range(rows):
        c0, c1 = code_ref[0, i], code_ref[1, i]
        straight = jnp.where(left, c0, c1)
        crossed = jnp.where(left, c1, c0)
        near = jnp.where(left, 0, 1)
        far = jnp.where(left, 2, -1)
        masks += [straight == near, crossed == near, straight == far, crossed == far]
    out_ref[rows * width :, :] = jnp.concatenate([m.astype(jnp.float32) for m in masks], axis=0)
    blocks.wait()


def left_kernel(width, groups, group_ref, code_ref, a_ref, p_ref, hi_ref, lo_ref):
    rows, per_row = group_ref.shape
    me = lax.axis_index("blk")
    odd = lax.axis_index("band") % 2
    pair = 2 * width
    wide = rows * width
    pt = p_ref[...].reshape(wide, pair).T
    row_of = lax.broadcasted_iota(jnp.int32, (1, wide), 1) // width
    codes = []
    for n in range(2):
        c = jnp.full((1, wide), code_ref[n, 0], jnp.int32)
        for i in range(1, rows):
            c = jnp.where(row_of == i, code_ref[n, i], c)
        codes.append(c)
    blocks = []
    for dest in (1, 2 - 2 * odd, 2 * odd):
        blocks.append(
            jnp.where(codes[0] == dest, pt[:width], 0.0) + jnp.where(codes[1] == dest, pt[width:], 0.0)
        )
    rt_hi, rt_lo = split(jnp.concatenate(blocks, axis=0))
    half = lax.broadcasted_iota(jnp.int32, (width, pair), 1) // width
    for p in range(rows // 2):
        tops = []
        for h in range(2):
            i = 2 * p + h
            cells = []
            for k in range(per_row):
                x = a_ref[i, :, (k // 2) * pair : (k // 2 + 1) * pair]
                if k % 2 != h:
                    x = pltpu.roll(x, width, 1)
                cells.append(jnp.where(half == h, x, 0.0))
            tops.append(cells)
        lanes = slice(p * pair, (p + 1) * pair)
        for j in range(groups):
            g = me ^ j
            parts = []
            for h in range(2):
                x = jnp.zeros((width, pair), jnp.float32)
                for k in range(per_row):
                    x = jnp.where(group_ref[2 * p + h, k] == g, tops[h][k], x)
                parts.append(x)
            b_hi, b_lo = split(jnp.concatenate(parts, axis=0))
            left = dot3(rt_hi[:, lanes], rt_lo[:, lanes], b_hi, b_lo)
            l_hi, l_lo = split(left)
            hi_ref[j, :, lanes] = l_hi
            lo_ref[j, :, lanes] = l_lo


def right_kernel(width, first, earlier_ref, group_ref, row_ref, hi_ref, lo_ref, *refs):
    sources, (own_ref, chip_ref, far_ref) = refs[:-3], refs[-3:]
    rows, per_row = group_ref.shape
    me = lax.axis_index("blk")
    pair = 2 * width
    pairs = len(sources) // 2
    right_half = lax.broadcasted_iota(jnp.int32, (width, pair), 1) >= width
    for q in range(pairs):
        found = []
        for j in (2 * q, 2 * q + 1):
            g = me ^ (first + j)
            src = sources[j]
            near, far = [], []
            for i in range(rows):
                s = jnp.int32(0)
                for k in range(per_row):
                    s = jnp.where(group_ref[i, k] == g, row_ref[i, k], s)
                x = src[pl.ds(pl.multiple_of(s * width, width), width), :]
                y = pltpu.roll(x, width, 1)
                m = [src[pl.ds(rows * width + 4 * s + t, 1), :] for t in range(4)]
                near.append(x * m[0] + y * m[1])
                far.append(x * m[2] + y * m[3])
            w = jnp.concatenate([jnp.concatenate(near, axis=0), jnp.concatenate(far, axis=0)], axis=1)
            w_hi, w_lo = split(w)
            found.append(dot3(hi_ref[first + j], lo_ref[first + j], w_hi, w_lo))
        swap = me % 2 == 1
        for t, out_ref in enumerate((own_ref, chip_ref, far_ref)):
            a, b = (f[t * width : (t + 1) * width] for f in found)
            before = jnp.where(swap, b, a)
            after = jnp.where(swap, a, b)
            for e in range(SHIFTS):
                tile = slice((e // 2) * pair, (e // 2 + 1) * pair)
                u, v = before[:, tile], after[:, tile]
                if e % 2 == 0:
                    v = pltpu.roll(v, width, 1)
                else:
                    u = pltpu.roll(u, width, 1)
                at = (e * pairs + q) * pair
                out_ref[:, at : at + pair] = jnp.where(right_half, v, u)


def add_kernel(groups, *refs):
    out_ref = refs[-1]
    me = lax.axis_index("blk")
    odd = lax.axis_index("band") % 2 == 1
    step = out_ref.shape[1] // 5
    pair = 2 * step // groups
    pairs = groups // 2 // CHUNKS
    for c in range(CHUNKS):
        own_ref, chip_ref, far_ref = refs[3 * c : 3 * c + 3]
        for q in range(pairs):
            place = ((me ^ (2 * (c * pairs + q))) // 2) * pair
            at = [slice((e * pairs + q) * pair, (e * pairs + q + 1) * pair) for e in range(SHIFTS)]
            own = [own_ref[:, t] for t in at]
            chip = [chip_ref[:, t] for t in at]
            far = [far_ref[:, t] for t in at]
            lower = [jnp.where(odd, u, v) for u, v in zip(chip, far)]
            upper = [jnp.where(odd, v, u) for u, v in zip(chip, far)]
            sums = [lower[0], lower[1] + own[0], lower[2] + own[1] + upper[0], own[2] + upper[1], upper[2]]
            for e in range(5):
                out_ref[:, pl.ds(pl.multiple_of(e * step + place, pair), pair)] = sums[e]


def body(fine_blocks, source_group, source_row, prolong_blocks, prolong_code):
    rows, width, pair = prolong_blocks.shape
    groups = lax.axis_size("blk")
    bands = lax.axis_size("band")
    f32 = jnp.float32
    prolong_code = prolong_code.T
    packed = pl.pallas_call(
        functools.partial(pack_kernel, width),
        out_shape=jax.ShapeDtypeStruct((rows * width + 4 * rows, pair), f32),
        in_specs=[pl.BlockSpec(memory_space=pltpu.HBM)] * 2,
        out_specs=vmem(),
        scratch_shapes=[pltpu.SMEM(prolong_code.shape, jnp.int32), pltpu.SemaphoreType.DMA((2,))],
        compiler_params=PARAMS,
        name="pack",
    )(prolong_code, prolong_blocks.reshape(rows * width, pair))
    arrived = [packed] + [
        lax.ppermute(packed, "blk", [(i, i ^ j) for i in range(groups)]) for j in range(1, groups)
    ]
    height = SHIFTS * width
    deep = rows * width
    hi, lo = pl.pallas_call(
        functools.partial(left_kernel, width, groups),
        out_shape=[jax.ShapeDtypeStruct((groups, height, deep), jnp.bfloat16)] * 2,
        in_specs=[smem(), smem(), vmem(), vmem()],
        out_specs=[vmem()] * 2,
        cost_estimate=pl.CostEstimate(
            flops=6 * groups * height * pair * deep, bytes_accessed=2000000, transcendentals=0
        ),
        compiler_params=PARAMS,
        name="left",
    )(source_group, prolong_code, fine_blocks, prolong_blocks)
    span = groups // CHUNKS
    parts = []
    own = packed
    for c in range(CHUNKS):
        own, chip, far = pl.pallas_call(
            functools.partial(right_kernel, width, c * span),
            out_shape=[jax.ShapeDtypeStruct((width, SHIFTS * span * width), f32)] * 3,
            in_specs=[pl.BlockSpec(memory_space=pl.ANY)] + [smem()] * 2 + [vmem()] * (2 + span),
            out_specs=[vmem()] * 3,
            cost_estimate=pl.CostEstimate(
                flops=6 * span * height * height * deep, bytes_accessed=2000000, transcendentals=0
            ),
            compiler_params=PARAMS,
            name=f"right_{c}",
        )(own, source_group, source_row, hi, lo, *arrived[c * span : (c + 1) * span])
        far = lax.ppermute(far, "band", [(i, (i + 1 if i % 2 else i - 1) % bands) for i in range(bands)])
        chip = lax.ppermute(chip, "band", [(i, i ^ 1) for i in range(bands)])
        parts += [own, chip, far]
    return pl.pallas_call(
        functools.partial(add_kernel, groups),
        out_shape=jax.ShapeDtypeStruct((width, 5 * groups * width), f32),
        in_specs=[vmem()] * len(parts),
        out_specs=vmem(),
        compiler_params=PARAMS,
        name="add",
    )(*parts)


def solution(mesh):
    return jax.shard_map(
        body,
        mesh=mesh,
        in_specs=(
            P(("blk", "band"), None, None),
            P(("blk", "band"), None),
            P(("blk", "band"), None),
            P(("blk", "band"), None, None),
            P(("blk", "band"), None),
        ),
        out_specs=P(("blk", "band"), None),
        check_vma=False,
    )
```

```python
import functools

import jax
import jax.numpy as jnp
from jax import lax
from jax.experimental import pallas as pl
from jax.experimental.pallas import tpu as pltpu
from jax.sharding import PartitionSpec as P

SHIFTS = 3
CHUNKS = 2
PARAMS = pltpu.CompilerParams(vmem_limit_bytes=24 * 1024 * 1024)


def vmem():
    return pl.BlockSpec(memory_space=pltpu.VMEM)


def smem():
    return pl.BlockSpec(memory_space=pltpu.SMEM)


def split(x):
    hi = x.astype(jnp.bfloat16)
    return hi, (x - hi.astype(jnp.float32)).astype(jnp.bfloat16)


def dot(a, b):
    return lax.dot_general(a, b, (((1,), (0,)), ((), ())), preferred_element_type=jnp.float32)


def dot3(a_hi, a_lo, b_hi, b_lo):
    return dot(a_hi, b_hi) + (dot(a_hi, b_lo) + dot(a_lo, b_hi))


def pack_kernel(width, code_hbm, p_hbm, out_hbm, code_ref, out_ref, sems):
    rows = code_ref.shape[1]
    n = 4
    size = rows * width // n
    codes = pltpu.make_async_copy(code_hbm, code_ref, sems.at[2 * n])
    codes.start()
    ins, outs = [], []
    for t in range(n):
        at = pl.ds(t * size, size)
        ins.append(pltpu.make_async_copy(p_hbm.at[at], out_ref.at[at], sems.at[t]))
        outs.append(pltpu.make_async_copy(out_ref.at[at], out_hbm.at[at], sems.at[n + t]))
        ins[t].start()
    codes.wait()
    lane = lax.broadcasted_iota(jnp.int32, (1, 2 * width), 1)
    left = lane < width
    masks = []
    for i in range(rows):
        c0, c1 = code_ref[0, i], code_ref[1, i]
        straight = jnp.where(left, c0, c1)
        crossed = jnp.where(left, c1, c0)
        near = jnp.where(left, 0, 1)
        far = jnp.where(left, 2, -1)
        masks += [straight == near, crossed == near, straight == far, crossed == far]
    out_ref[rows * width :, :] = jnp.concatenate([m.astype(jnp.float32) for m in masks], axis=0)
    tail = pl.ds(rows * width, 4 * rows)
    outs.append(pltpu.make_async_copy(out_ref.at[tail], out_hbm.at[tail], sems.at[2 * n + 1]))
    outs[n].start()
    for t in range(n):
        ins[t].wait()
        outs[t].start()
    for out in outs:
        out.wait()


def left_kernel(width, group_ref, row_ref, code_ref, a_ref, p_ref, hi_ref, lo_ref, b_hi_ref, b_lo_ref):
    rows, per_row = group_ref.shape
    groups = hi_ref.shape[0]
    me = lax.axis_index("blk")
    odd = lax.axis_index("band") % 2
    pair = 2 * width
    wide = rows * width
    b_hi_ref[...] = jnp.zeros_like(b_hi_ref)
    b_lo_ref[...] = jnp.zeros_like(b_lo_ref)
    half = lax.broadcasted_iota(jnp.int32, (width, pair), 1) // width
    for i in range(rows):
        for k in range(per_row):
            x = a_ref[i, :, (k // 2) * pair : (k // 2 + 1) * pair]
            s = row_ref[i, k]
            turned = pltpu.roll(x, width, 1)
            x = jnp.where(half == s % 2, jnp.where(s % 2 == k % 2, x, turned), 0.0)
            x_hi, x_lo = split(x)
            j = group_ref[i, k] ^ me
            at = pl.ds(pl.multiple_of((s // 2) * pair, pair), pair)
            b_hi_ref[j, i * width : (i + 1) * width, at] = x_hi
            b_lo_ref[j, i * width : (i + 1) * width, at] = x_lo
    pt = p_ref[...].reshape(wide, pair).T
    row_of = lax.broadcasted_iota(jnp.int32, (1, wide), 1) // width
    codes = []
    for n in range(2):
        c = jnp.full((1, wide), code_ref[n, 0], jnp.int32)
        for i in range(1, rows):
            c = jnp.where(row_of == i, code_ref[n, i], c)
        codes.append(c)
    blocks = []
    for dest in (1, 2 - 2 * odd, 2 * odd):
        blocks.append(
            jnp.where(codes[0] == dest, pt[:width], 0.0) + jnp.where(codes[1] == dest, pt[width:], 0.0)
        )
    rt_hi, rt_lo = split(jnp.concatenate(blocks, axis=0))
    for j in range(groups):
        hi_ref[j], lo_ref[j] = split(dot3(rt_hi, rt_lo, b_hi_ref[j], b_lo_ref[j]))


def spread(src, rows, width):
    near, far = [], []
    for s in range(rows):
        x = src[s * width : (s + 1) * width, :]
        y = pltpu.roll(x, width, 1)
        at = rows * width + 4 * s
        m = [src[at + t : at + t + 1, :] for t in range(4)]
        near.append(x * m[0] + y * m[1])
        far.append(x * m[2] + y * m[3])
    return jnp.concatenate([jnp.concatenate(near, axis=0), jnp.concatenate(far, axis=0)], axis=1)


def right_kernel(width, first, earlier_ref, hi_ref, lo_ref, *refs):
    sources, (own_ref, chip_ref, far_ref) = refs[:-3], refs[-3:]
    rows = hi_ref.shape[2] // width
    me = lax.axis_index("blk")
    pair = 2 * width
    pairs = len(sources) // 2
    right_half = lax.broadcasted_iota(jnp.int32, (width, pair), 1) >= width
    for q in range(pairs):
        found = []
        for j in (2 * q, 2 * q + 1):
            w_hi, w_lo = split(spread(sources[j], rows, width))
            found.append(dot3(hi_ref[first + j], lo_ref[first + j], w_hi, w_lo))
        swap = me % 2 == 1
        for t, out_ref in enumerate((own_ref, chip_ref, far_ref)):
            a, b = (f[t * width : (t + 1) * width] for f in found)
            before = jnp.where(swap, b, a)
            after = jnp.where(swap, a, b)
            for e in range(SHIFTS):
                tile = slice((e // 2) * pair, (e // 2 + 1) * pair)
                u, v = before[:, tile], after[:, tile]
                if e % 2 == 0:
                    v = pltpu.roll(v, width, 1)
                else:
                    u = pltpu.roll(u, width, 1)
                at = (e * pairs + q) * pair
                out_ref[:, at : at + pair] = jnp.where(right_half, v, u)


def add_kernel(groups, *refs):
    out_ref = refs[-1]
    me = lax.axis_index("blk")
    odd = lax.axis_index("band") % 2 == 1
    step = out_ref.shape[1] // 5
    pair = 2 * step // groups
    pairs = groups // 2 // CHUNKS
    for c in range(CHUNKS):
        own_ref, far_ref, chip_ref = refs[3 * c : 3 * c + 3]
        for q in range(pairs):
            place = ((me ^ (2 * (c * pairs + q))) // 2) * pair
            at = [slice((e * pairs + q) * pair, (e * pairs + q + 1) * pair) for e in range(SHIFTS)]
            own = [own_ref[:, t] for t in at]
            chip = [chip_ref[:, t] for t in at]
            far = [far_ref[:, t] for t in at]
            lower = [jnp.where(odd, u, v) for u, v in zip(chip, far)]
            upper = [jnp.where(odd, v, u) for u, v in zip(chip, far)]
            sums = [lower[0], lower[1] + own[0], lower[2] + own[1] + upper[0], own[2] + upper[1], upper[2]]
            for e in range(5):
                out_ref[:, pl.ds(pl.multiple_of(e * step + place, pair), pair)] = sums[e]


def body(fine_blocks, source_group, source_row, prolong_blocks, prolong_code):
    rows, width, pair = prolong_blocks.shape
    groups = lax.axis_size("blk")
    bands = lax.axis_size("band")
    f32 = jnp.float32
    prolong_code = prolong_code.T
    packed = pl.pallas_call(
        functools.partial(pack_kernel, width),
        out_shape=jax.ShapeDtypeStruct((rows * width + 4 * rows, pair), f32),
        in_specs=[pl.BlockSpec(memory_space=pltpu.HBM)] * 2,
        out_specs=pl.BlockSpec(memory_space=pl.ANY),
        scratch_shapes=[
            pltpu.SMEM(prolong_code.shape, jnp.int32),
            pltpu.VMEM((rows * width + 4 * rows, pair), f32),
            pltpu.SemaphoreType.DMA((2 * 4 + 2,)),
        ],
        compiler_params=pltpu.CompilerParams(vmem_limit_bytes=60 * 1024 * 1024),
        name="pack",
    )(prolong_code, prolong_blocks.reshape(rows * width, pair))
    arrived = [packed] + [
        lax.ppermute(packed, "blk", [(i, i ^ j) for i in range(groups)]) for j in range(1, groups)
    ]
    height = SHIFTS * width
    deep = rows * width
    hi, lo = pl.pallas_call(
        functools.partial(left_kernel, width),
        out_shape=[jax.ShapeDtypeStruct((groups, height, deep), jnp.bfloat16)] * 2,
        in_specs=[smem()] * 3 + [vmem()] * 2,
        out_specs=[vmem()] * 2,
        scratch_shapes=[pltpu.VMEM((groups, deep, deep), jnp.bfloat16)] * 2,
        cost_estimate=pl.CostEstimate(
            flops=6 * groups * height * deep * deep, bytes_accessed=2000000, transcendentals=0
        ),
        compiler_params=PARAMS,
        name="left",
    )(source_group, source_row, prolong_code, fine_blocks, prolong_blocks)
    span = groups // CHUNKS
    parts = []
    own = packed
    for c in range(CHUNKS):
        shape = (width, SHIFTS * span * width)
        own, chip, far = pl.pallas_call(
            functools.partial(right_kernel, width, c * span),
            out_shape=[
                jax.ShapeDtypeStruct(shape, f32),
                jax.ShapeDtypeStruct(shape, f32),
                jax.ShapeDtypeStruct(shape, f32),
            ],
            in_specs=[pl.BlockSpec(memory_space=pl.ANY)] + [vmem()] * (2 + span),
            out_specs=[vmem()] * 3,
            cost_estimate=pl.CostEstimate(
                flops=6 * span * height * height * deep, bytes_accessed=2000000, transcendentals=0
            ),
            compiler_params=PARAMS,
            name=f"right_{c}",
        )(own, hi, lo, *arrived[c * span : (c + 1) * span])
        far = lax.ppermute(far, "band", [(i, (i + 1 if i % 2 else i - 1) % bands) for i in range(bands)])
        chip = lax.ppermute(chip, "band", [(i, i ^ 1) for i in range(bands)])
        parts += [own, far, chip]
    return pl.pallas_call(
        functools.partial(add_kernel, groups),
        out_shape=jax.ShapeDtypeStruct((width, 5 * groups * width), f32),
        in_specs=[vmem()] * len(parts),
        out_specs=vmem(),
        compiler_params=PARAMS,
        name="add",
    )(*parts)


def solution(mesh):
    return jax.shard_map(
        body,
        mesh=mesh,
        in_specs=(
            P(("blk", "band"), None, None),
            P(("blk", "band"), None),
            P(("blk", "band"), None),
            P(("blk", "band"), None, None),
            P(("blk", "band"), None),
        ),
        out_specs=P(("blk", "band"), None),
        check_vma=False,
    )
```

```python
import functools

import jax
import jax.numpy as jnp
from jax import lax
from jax.experimental import pallas as pl
from jax.experimental.pallas import tpu as pltpu
from jax.sharding import PartitionSpec as P

SHIFTS = 3
CHUNKS = 2
PARAMS = pltpu.CompilerParams(vmem_limit_bytes=24 * 1024 * 1024)


def vmem():
    return pl.BlockSpec(memory_space=pltpu.VMEM)


def smem():
    return pl.BlockSpec(memory_space=pltpu.SMEM)


def split(x):
    hi = x.astype(jnp.bfloat16)
    return hi, (x - hi.astype(jnp.float32)).astype(jnp.bfloat16)


def dot(a, b):
    return lax.dot_general(a, b, (((1,), (0,)), ((), ())), preferred_element_type=jnp.float32)


def dot3(a_hi, a_lo, b_hi, b_lo):
    return dot(a_hi, b_hi) + (dot(a_hi, b_lo) + dot(a_lo, b_hi))


def lanes_kernel(out_ref):
    pair = out_ref.shape[1]
    out_ref[...] = lax.broadcasted_iota(jnp.int32, out_ref.shape, 1) // (pair // 2)


def pack_kernel(width, lanes_ref, code_ref, p_ref, out_ref):
    deep = p_ref.shape[0]
    rows = deep // width
    out_ref[:deep, :] = p_ref[...]
    left = lanes_ref[...] == 0
    straight = [jnp.where(left, code_ref[0:1, i : i + 1], code_ref[1:2, i : i + 1]) for i in range(rows)]
    crossed = [jnp.where(left, code_ref[1:2, i : i + 1], code_ref[0:1, i : i + 1]) for i in range(rows)]
    out_ref[deep:, :] = jnp.concatenate(straight + crossed, axis=0).astype(jnp.float32)


def left_kernel(width, group_ref, row_ref, code_ref, a_ref, p_ref, hi_ref, lo_ref, b_hi_ref, b_lo_ref):
    rows, per_row = group_ref.shape
    groups = hi_ref.shape[0]
    me = lax.axis_index("blk")
    odd = lax.axis_index("band") % 2
    pair = 2 * width
    wide = rows * width
    b_hi_ref[...] = jnp.zeros_like(b_hi_ref)
    b_lo_ref[...] = jnp.zeros_like(b_lo_ref)
    half = lax.broadcasted_iota(jnp.int32, (width, pair), 1) // width
    for i in range(rows):
        for k in range(per_row):
            x = a_ref[i, :, (k // 2) * pair : (k // 2 + 1) * pair]
            s = row_ref[i, k]
            turned = pltpu.roll(x, width, 1)
            x = jnp.where(half == s % 2, jnp.where(s % 2 == k % 2, x, turned), 0.0)
            x_hi, x_lo = split(x)
            j = group_ref[i, k] ^ me
            at = pl.ds(pl.multiple_of((s // 2) * pair, pair), pair)
            b_hi_ref[j, i * width : (i + 1) * width, at] = x_hi
            b_lo_ref[j, i * width : (i + 1) * width, at] = x_lo
    pt = p_ref[...].reshape(wide, pair).T
    row_of = lax.broadcasted_iota(jnp.int32, (1, wide), 1) // width
    codes = []
    for n in range(2):
        c = jnp.full((1, wide), code_ref[n, 0], jnp.int32)
        for i in range(1, rows):
            c = jnp.where(row_of == i, code_ref[n, i], c)
        codes.append(c)
    blocks = []
    for dest in (1, 2 - 2 * odd, 2 * odd):
        blocks.append(
            jnp.where(codes[0] == dest, pt[:width], 0.0) + jnp.where(codes[1] == dest, pt[width:], 0.0)
        )
    rt_hi, rt_lo = split(jnp.concatenate(blocks, axis=0))
    for j in range(groups):
        hi_ref[j], lo_ref[j] = split(dot3(rt_hi, rt_lo, b_hi_ref[j], b_lo_ref[j]))


def spread(src, rows, width):
    lane = lax.broadcasted_iota(jnp.int32, (1, 2 * width), 1)
    low = jnp.where(lane < width, 0.0, 1.0)
    high = jnp.where(lane < width, 2.0, -1.0)
    deep = rows * width
    near, far = [], []
    for s in range(rows):
        x = src[s * width : (s + 1) * width, :]
        y = pltpu.roll(x, width, 1)
        straight = src[deep + s : deep + s + 1, :]
        crossed = src[deep + rows + s : deep + rows + s + 1, :]
        near.append(jnp.where(straight == low, x, 0.0) + jnp.where(crossed == low, y, 0.0))
        far.append(jnp.where(straight == high, x, 0.0) + jnp.where(crossed == high, y, 0.0))
    return jnp.concatenate([jnp.concatenate(near, axis=0), jnp.concatenate(far, axis=0)], axis=1)


def right_kernel(width, first, earlier_ref, hi_ref, lo_ref, *refs):
    sources, (own_ref, chip_ref, far_ref) = refs[:-3], refs[-3:]
    rows = hi_ref.shape[2] // width
    me = lax.axis_index("blk")
    pair = 2 * width
    pairs = len(sources) // 2
    right_half = lax.broadcasted_iota(jnp.int32, (width, pair), 1) >= width
    for q in range(pairs):
        found = []
        for j in (2 * q, 2 * q + 1):
            w_hi, w_lo = split(spread(sources[j], rows, width))
            found.append(dot3(hi_ref[first + j], lo_ref[first + j], w_hi, w_lo))
        swap = me % 2 == 1
        for t, out_ref in enumerate((own_ref, chip_ref, far_ref)):
            a, b = (f[t * width : (t + 1) * width] for f in found)
            before = jnp.where(swap, b, a)
            after = jnp.where(swap, a, b)
            for e in range(SHIFTS):
                tile = slice((e // 2) * pair, (e // 2 + 1) * pair)
                u, v = before[:, tile], after[:, tile]
                if e % 2 == 0:
                    v = pltpu.roll(v, width, 1)
                else:
                    u = pltpu.roll(u, width, 1)
                at = (e * pairs + q) * pair
                out_ref[:, at : at + pair] = jnp.where(right_half, v, u)


def add_kernel(groups, *refs):
    out_ref = refs[-1]
    me = lax.axis_index("blk")
    odd = lax.axis_index("band") % 2 == 1
    step = out_ref.shape[1] // 5
    pair = 2 * step // groups
    pairs = groups // 2 // CHUNKS
    for c in range(CHUNKS):
        own_ref, far_ref, chip_ref = refs[3 * c : 3 * c + 3]
        for q in range(pairs):
            place = ((me ^ (2 * (c * pairs + q))) // 2) * pair
            at = [slice((e * pairs + q) * pair, (e * pairs + q + 1) * pair) for e in range(SHIFTS)]
            own = [own_ref[:, t] for t in at]
            chip = [chip_ref[:, t] for t in at]
            far = [far_ref[:, t] for t in at]
            lower = [jnp.where(odd, u, v) for u, v in zip(chip, far)]
            upper = [jnp.where(odd, v, u) for u, v in zip(chip, far)]
            sums = [lower[0], lower[1] + own[0], lower[2] + own[1] + upper[0], own[2] + upper[1], upper[2]]
            for e in range(5):
                out_ref[:, pl.ds(pl.multiple_of(e * step + place, pair), pair)] = sums[e]


def body(fine_blocks, source_group, source_row, prolong_blocks, prolong_code):
    rows, width, pair = prolong_blocks.shape
    groups = lax.axis_size("blk")
    bands = lax.axis_size("band")
    f32 = jnp.float32
    prolong_code = prolong_code.T
    lanes = pl.pallas_call(
        lanes_kernel,
        out_shape=jax.ShapeDtypeStruct((1, pair), jnp.int32),
        out_specs=vmem(),
        cost_estimate=pl.CostEstimate(flops=4000000000, bytes_accessed=10000000, transcendentals=0),
        compiler_params=PARAMS,
        name="lanes",
    )()
    packed = pl.pallas_call(
        functools.partial(pack_kernel, width),
        out_shape=jax.ShapeDtypeStruct((rows * width + 2 * rows, pair), f32),
        in_specs=[vmem()] * 3,
        out_specs=vmem(),
        compiler_params=PARAMS,
        name="pack",
    )(lanes, prolong_code, prolong_blocks.reshape(rows * width, pair))
    arrived = [packed] + [
        lax.ppermute(packed, "blk", [(i, i ^ j) for i in range(groups)]) for j in range(1, groups)
    ]
    height = SHIFTS * width
    deep = rows * width
    hi, lo = pl.pallas_call(
        functools.partial(left_kernel, width),
        out_shape=[jax.ShapeDtypeStruct((groups, height, deep), jnp.bfloat16)] * 2,
        in_specs=[smem()] * 3 + [vmem()] * 2,
        out_specs=[vmem()] * 2,
        scratch_shapes=[pltpu.VMEM((groups, deep, deep), jnp.bfloat16)] * 2,
        cost_estimate=pl.CostEstimate(
            flops=6 * groups * height * deep * deep, bytes_accessed=2000000, transcendentals=0
        ),
        compiler_params=PARAMS,
        name="left",
    )(source_group, source_row, prolong_code, fine_blocks, prolong_blocks)
    span = groups // CHUNKS
    parts = []
    own = packed
    for c in range(CHUNKS):
        shape = (width, SHIFTS * span * width)
        own, chip, far = pl.pallas_call(
            functools.partial(right_kernel, width, c * span),
            out_shape=[
                jax.ShapeDtypeStruct(shape, f32),
                jax.ShapeDtypeStruct(shape, f32),
                jax.ShapeDtypeStruct(shape, f32),
            ],
            in_specs=[pl.BlockSpec(memory_space=pl.ANY)] + [vmem()] * (2 + span),
            out_specs=[vmem()] * 3,
            cost_estimate=pl.CostEstimate(
                flops=6 * span * height * height * deep, bytes_accessed=2000000, transcendentals=0
            ),
            compiler_params=PARAMS,
            name=f"right_{c}",
        )(own, hi, lo, *arrived[c * span : (c + 1) * span])
        far = lax.ppermute(far, "band", [(i, (i + 1 if i % 2 else i - 1) % bands) for i in range(bands)])
        chip = lax.ppermute(chip, "band", [(i, i ^ 1) for i in range(bands)])
        parts += [own, far, chip]
    return pl.pallas_call(
        functools.partial(add_kernel, groups),
        out_shape=jax.ShapeDtypeStruct((width, 5 * groups * width), f32),
        in_specs=[vmem()] * len(parts),
        out_specs=vmem(),
        compiler_params=PARAMS,
        name="add",
    )(*parts)


def solution(mesh):
    return jax.shard_map(
        body,
        mesh=mesh,
        in_specs=(
            P(("blk", "band"), None, None),
            P(("blk", "band"), None),
            P(("blk", "band"), None),
            P(("blk", "band"), None, None),
            P(("blk", "band"), None),
        ),
        out_specs=P(("blk", "band"), None),
        check_vma=False,
    )
```

```python
import functools

import jax
import jax.numpy as jnp
from jax import lax
from jax.experimental import pallas as pl
from jax.experimental.pallas import tpu as pltpu
from jax.sharding import PartitionSpec as P

SHIFTS = 3
LAG = 1
PARAMS = pltpu.CompilerParams(vmem_limit_bytes=24 * 1024 * 1024)


def vmem():
    return pl.BlockSpec(memory_space=pltpu.VMEM)


def smem():
    return pl.BlockSpec(memory_space=pltpu.SMEM)


def split(x):
    hi = x.astype(jnp.bfloat16)
    return hi, (x - hi.astype(jnp.float32)).astype(jnp.bfloat16)


def dot(a, b):
    return lax.dot_general(a, b, (((1,), (0,)), ((), ())), preferred_element_type=jnp.float32)


def dot3(a_hi, a_lo, b_hi, b_lo):
    return dot(a_hi, b_hi) + (dot(a_hi, b_lo) + dot(a_lo, b_hi))


def lanes_kernel(out_ref):
    pair = out_ref.shape[1]
    out_ref[...] = lax.broadcasted_iota(jnp.int32, out_ref.shape, 1) // (pair // 2)


def pack_kernel(width, lanes_ref, code_ref, p_ref, out_ref):
    deep = p_ref.shape[0]
    rows = deep // width
    out_ref[:deep, :] = p_ref[...]
    left = lanes_ref[...] == 0
    straight = [jnp.where(left, code_ref[0:1, i : i + 1], code_ref[1:2, i : i + 1]) for i in range(rows)]
    crossed = [jnp.where(left, code_ref[1:2, i : i + 1], code_ref[0:1, i : i + 1]) for i in range(rows)]
    out_ref[deep:, :] = jnp.concatenate(straight + crossed, axis=0).astype(jnp.float32)


def left_kernel(width, group_ref, row_ref, code_ref, a_ref, packed_ref, hi_ref, lo_ref, b_hi_ref, b_lo_ref):
    rows, per_row = group_ref.shape
    groups = hi_ref.shape[0]
    me = lax.axis_index("blk")
    odd = lax.axis_index("band") % 2
    pair = 2 * width
    wide = rows * width
    b_hi_ref[...] = jnp.zeros_like(b_hi_ref)
    b_lo_ref[...] = jnp.zeros_like(b_lo_ref)
    half = lax.broadcasted_iota(jnp.int32, (width, pair), 1) // width
    for i in range(rows):
        for k in range(per_row):
            x = a_ref[i, :, (k // 2) * pair : (k // 2 + 1) * pair]
            s = row_ref[i, k]
            turned = pltpu.roll(x, width, 1)
            x = jnp.where(half == s % 2, jnp.where(s % 2 == k % 2, x, turned), 0.0)
            x_hi, x_lo = split(x)
            j = group_ref[i, k] ^ me
            at = pl.ds(pl.multiple_of((s // 2) * pair, pair), pair)
            b_hi_ref[j, i * width : (i + 1) * width, at] = x_hi
            b_lo_ref[j, i * width : (i + 1) * width, at] = x_lo
    pt = packed_ref[:wide, :].T
    row_of = lax.broadcasted_iota(jnp.int32, (1, wide), 1) // width
    codes = []
    for n in range(2):
        c = jnp.full((1, wide), code_ref[n, 0], jnp.int32)
        for i in range(1, rows):
            c = jnp.where(row_of == i, code_ref[n, i], c)
        codes.append(c)
    blocks = []
    for dest in (1, 2 - 2 * odd, 2 * odd):
        blocks.append(
            jnp.where(codes[0] == dest, pt[:width], 0.0) + jnp.where(codes[1] == dest, pt[width:], 0.0)
        )
    rt_hi, rt_lo = split(jnp.concatenate(blocks, axis=0))
    for j in range(groups):
        hi_ref[j], lo_ref[j] = split(dot3(rt_hi, rt_lo, b_hi_ref[j], b_lo_ref[j]))


def spread(src, rows, width):
    lane = lax.broadcasted_iota(jnp.int32, (1, 2 * width), 1)
    low = jnp.where(lane < width, 0.0, 1.0)
    high = jnp.where(lane < width, 2.0, -1.0)
    base = rows * width
    near, far = [], []
    for s in range(rows):
        x = src[s * width : (s + 1) * width, :]
        y = pltpu.roll(x, width, 1)
        straight = src[base + s : base + s + 1, :]
        crossed = src[base + rows + s : base + rows + s + 1, :]
        near.append(jnp.where(straight == low, x, 0.0) + jnp.where(crossed == low, y, 0.0))
        far.append(jnp.where(straight == high, x, 0.0) + jnp.where(crossed == high, y, 0.0))
    return jnp.concatenate([jnp.concatenate(near, axis=0), jnp.concatenate(far, axis=0)], axis=1)


def multiply(hi_ref, lo_ref, slot, src, width):
    rows = hi_ref.shape[2] // width
    return dot3(hi_ref[slot], lo_ref[slot], *split(spread(src, rows, width)))


def lay_out(found, outs, width):
    swap = lax.axis_index("blk") % 2 == 1
    pair = 2 * width
    pairs = len(found) // 2
    right_half = lax.broadcasted_iota(jnp.int32, (width, pair), 1) >= width
    for q in range(pairs):
        for t, out_ref in enumerate(outs):
            a, b = (f[t * width : (t + 1) * width] for f in found[2 * q : 2 * q + 2])
            before = jnp.where(swap, b, a)
            after = jnp.where(swap, a, b)
            for e in range(SHIFTS):
                tile = slice((e // 2) * pair, (e // 2 + 1) * pair)
                u, v = before[:, tile], after[:, tile]
                if e % 2 == 0:
                    v = pltpu.roll(v, width, 1)
                else:
                    u = pltpu.roll(u, width, 1)
                at = (e * pairs + q) * pair
                out_ref[:, at : at + pair] = jnp.where(right_half, v, u)


def near_kernel(width, hi_ref, lo_ref, *refs):
    lay_out([multiply(hi_ref, lo_ref, j, src, width) for j, src in enumerate(refs[:-3])], refs[-3:], width)


def product_kernel(width, first, turn, earlier_ref, hi_ref, lo_ref, *refs):
    sources, out_ref = refs[:-1], refs[-1]

    @pl.when(lax.axis_index("band") % 2 == turn)
    def _():
        for j, src in enumerate(sources):
            out_ref[j] = multiply(hi_ref, lo_ref, first + j, src, width)


def join_kernel(width, turn, hi_ref, lo_ref, found_ref, last_ref, *refs):
    handed, outs = refs[:-3], refs[-3:]
    mine = lax.axis_index("band") % 2 == turn

    @pl.when(mine)
    def _():
        found = [found_ref[j] for j in range(found_ref.shape[0])]
        found.append(multiply(hi_ref, lo_ref, hi_ref.shape[0] - 1, last_ref, width))
        lay_out(found, outs, width)

    @pl.when(jnp.logical_not(mine))
    def _():
        for out_ref in outs[: 3 - len(handed)]:
            out_ref[...] = jnp.zeros_like(out_ref)
        for out_ref, given_ref in zip(outs[3 - len(handed) :], handed):
            out_ref[...] = given_ref[...]


def place(sum_ref, part_ref, groups, first, shift):
    me = lax.axis_index("blk")
    pair = 2 * part_ref.shape[0]
    pairs = part_ref.shape[1] // (SHIFTS * pair)
    for q in range(pairs):
        tile = (me ^ (first + 2 * q)) // 2
        for e in range(SHIFTS):
            at = pl.ds(pl.multiple_of(((e + shift) * (groups // 2) + tile) * pair, pair), pair)
            sum_ref[:, at] += part_ref[:, (e * pairs + q) * pair : (e * pairs + q + 1) * pair]


def first_kernel(groups, near_ref, far_ref, out_ref):
    out_ref[...] = jnp.zeros_like(out_ref)
    place(out_ref, near_ref, groups, 0, 1)
    place(out_ref, far_ref, groups, 0, 2 * (lax.axis_index("band") % 2))


def early_kernel(groups, first_ref, rest_ref, up_ref, out_ref):
    span = groups // 2
    out_ref[...] = first_ref[...]
    place(out_ref, rest_ref, groups, span, 1)
    place(out_ref, up_ref, groups, span * (1 - lax.axis_index("band") % 2), 0)


def late_kernel(groups, early_ref, down_ref, chip_ref, out_ref):
    odd = lax.axis_index("band") % 2
    span = groups // 2
    out_ref[...] = early_ref[...]
    place(out_ref, chip_ref, groups, span, 2 - 2 * odd)
    place(out_ref, down_ref, groups, span * odd, 2)


def body(fine_blocks, source_group, source_row, prolong_blocks, prolong_code):
    rows, width, pair = prolong_blocks.shape
    groups = lax.axis_size("blk")
    bands = lax.axis_size("band")
    f32 = jnp.float32
    prolong_code = prolong_code.T
    lanes = pl.pallas_call(
        lanes_kernel,
        out_shape=jax.ShapeDtypeStruct((1, pair), jnp.int32),
        out_specs=vmem(),
        cost_estimate=pl.CostEstimate(flops=4000000000, bytes_accessed=10000000, transcendentals=0),
        compiler_params=PARAMS,
        name="lanes",
    )()
    packed = pl.pallas_call(
        functools.partial(pack_kernel, width),
        out_shape=jax.ShapeDtypeStruct((rows * width + 2 * rows, pair), f32),
        in_specs=[vmem()] * 3,
        out_specs=vmem(),
        compiler_params=PARAMS,
        name="pack",
    )(lanes, prolong_code, prolong_blocks.reshape(rows * width, pair))
    height = SHIFTS * width
    deep = rows * width

    def call(kernel, name, shapes, dtype=f32, inputs=0, **more):
        more.setdefault("in_specs", [vmem()] * inputs)
        single = not isinstance(shapes, list)
        out = [jax.ShapeDtypeStruct(x, dtype) for x in ([shapes] if single else shapes)]
        return pl.pallas_call(
            kernel,
            out_shape=out[0] if single else out,
            out_specs=vmem() if single else [vmem()] * len(out),
            compiler_params=PARAMS,
            name=name,
            **more,
        )

    def gather(offsets):
        to = []
        for b in range(groups):
            for r in range(bands):
                offset = offsets[r % 2]
                other = (b, r ^ 2) if offset is None else (b ^ offset, r)
                to.append((b * bands + r, other[0] * bands + other[1]))
        return lax.ppermute(packed, ("blk", "band"), to)

    span = groups // 2
    sources = [packed] + [gather((j, j)) for j in range(1, span)]
    odd_steps = [*range(span, groups)] + [None] * LAG
    even_steps = [None] * LAG + [*range(span, groups)]
    rest = [gather(offsets) for offsets in zip(even_steps, odd_steps)]
    hi, lo = pl.pallas_call(
        functools.partial(left_kernel, width),
        out_shape=[jax.ShapeDtypeStruct((groups, height, deep), jnp.bfloat16)] * 2,
        in_specs=[smem()] * 3 + [vmem()] * 2,
        out_specs=[vmem()] * 2,
        scratch_shapes=[pltpu.VMEM((groups, deep, deep), jnp.bfloat16)] * 2,
        cost_estimate=pl.CostEstimate(
            flops=6 * groups * height * deep * deep, bytes_accessed=2000000, transcendentals=0
        ),
        compiler_params=PARAMS,
        name="left",
    )(source_group, source_row, prolong_code, fine_blocks, packed)

    def products(name, turn, sources, earlier):
        kernel = functools.partial(product_kernel, width, span, turn)
        specs = [pl.BlockSpec(memory_space=pl.ANY)] + [vmem()] * (2 + len(sources))
        shape = (len(sources), height, 2 * pair)
        return call(kernel, name, shape, in_specs=specs)(earlier, hi, lo, *sources)

    parts = [(width, SHIFTS * span * width)] * 3

    def join(name, turn, found, last, *handed):
        kernel = functools.partial(join_kernel, width, turn)
        return call(kernel, name, parts, inputs=4 + len(handed))(hi, lo, found, last, *handed)

    own_near, chip_near, far = call(
        functools.partial(near_kernel, width), "near", parts, inputs=2 + span
    )(hi, lo, *sources)
    far = lax.ppermute(far, "band", [(i, (i + 1 if i % 2 else i - 1) % bands) for i in range(bands)])
    found = products("rest_odd", 1, rest[: span - 1], own_near)
    own, chip, up = join("join_odd", 1, found, rest[span - 1], chip_near)
    up = lax.ppermute(up, "band", [(i, (i + 1) % bands) for i in range(bands)])
    found = products("rest_even", 0, rest[LAG : LAG + span - 1], own)
    own, chip, down = join("join_even", 0, found, rest[-1], own, chip, chip_near)
    down = lax.ppermute(down, "band", [((i + 1) % bands, i) for i in range(bands)])
    chip = lax.ppermute(chip, "band", [(i, i ^ 1) for i in range(bands)])
    whole = (width, 5 * groups * width)
    slow = pl.CostEstimate(flops=4000000000, bytes_accessed=2000000, transcendentals=0)
    first = call(functools.partial(first_kernel, groups), "first", whole, inputs=2)(own_near, far)
    early = call(functools.partial(early_kernel, groups), "early", whole, inputs=3, cost_estimate=slow)(
        first, own, up
    )
    return call(functools.partial(late_kernel, groups), "late", whole, inputs=3)(early, down, chip)


def solution(mesh):
    return jax.shard_map(
        body,
        mesh=mesh,
        in_specs=(
            P(("blk", "band"), None, None),
            P(("blk", "band"), None),
            P(("blk", "band"), None),
            P(("blk", "band"), None, None),
            P(("blk", "band"), None),
        ),
        out_specs=P(("blk", "band"), None),
        check_vma=False,
    )
```

```python
import functools

import jax
import jax.numpy as jnp
from jax import lax
from jax.experimental import pallas as pl
from jax.experimental.pallas import tpu as pltpu
from jax.sharding import PartitionSpec as P

SHIFTS = 3
LAG = 1
PARAMS = pltpu.CompilerParams(vmem_limit_bytes=24 * 1024 * 1024)


def vmem():
    return pl.BlockSpec(memory_space=pltpu.VMEM)


def split(x):
    hi = x.astype(jnp.bfloat16)
    return hi, (x - hi.astype(jnp.float32)).astype(jnp.bfloat16)


def dot(a, b):
    return lax.dot_general(a, b, (((1,), (0,)), ((), ())), preferred_element_type=jnp.float32)


def dot3(a_hi, a_lo, b_hi, b_lo):
    return dot(a_hi, b_hi) + (dot(a_hi, b_lo) + dot(a_lo, b_hi))


def lanes_kernel(out_ref):
    pair = out_ref.shape[1]
    out_ref[...] = lax.broadcasted_iota(jnp.int32, out_ref.shape, 1) // (pair // 2)


def pack_kernel(width, lanes_ref, code_ref, p_ref, out_ref):
    deep = p_ref.shape[0]
    rows = deep // width
    out_ref[:deep, :] = p_ref[...]
    left = lanes_ref[...] == 0
    straight = [jnp.where(left, code_ref[0:1, i : i + 1], code_ref[1:2, i : i + 1]) for i in range(rows)]
    crossed = [jnp.where(left, code_ref[1:2, i : i + 1], code_ref[0:1, i : i + 1]) for i in range(rows)]
    out_ref[deep:, :] = jnp.concatenate(straight + crossed, axis=0).astype(jnp.float32)


def left_kernel(width, group_ref, row_ref, code_ref, a_ref, packed_ref, hi_ref, lo_ref):
    rows, per_row = group_ref.shape
    groups = hi_ref.shape[0]
    me = lax.axis_index("blk")
    odd = lax.axis_index("band") % 2
    pair = 2 * width
    wide = rows * width
    lane_block = lax.broadcasted_iota(jnp.int32, (rows, wide), 1) // width
    pt = packed_ref[:wide, :].T
    row_of = lane_block[:1]
    codes = []
    for n in range(2):
        c = jnp.broadcast_to(code_ref[n : n + 1, :1], (1, wide))
        for i in range(1, rows):
            c = jnp.where(row_of == i, code_ref[n : n + 1, i : i + 1], c)
        codes.append(c)
    blocks = []
    for dest in (1, 2 - 2 * odd, 2 * odd):
        blocks.append(
            jnp.where(codes[0] == dest, pt[:width], 0.0) + jnp.where(codes[1] == dest, pt[width:], 0.0)
        )
    rt_hi, rt_lo = split(jnp.concatenate(blocks, axis=0))
    left_half = lax.broadcasted_iota(jnp.int32, (width, pair), 1) < width
    twice = []
    for i in range(rows):
        for k in range(0, per_row, 2):
            x = a_ref[i, :, (k // 2) * pair : (k // 2 + 1) * pair]
            y = pltpu.roll(x, width, 1)
            twice += [jnp.where(left_half, x, y), jnp.where(left_half, y, x)]
    slots = [group_ref[:, k : k + 1] ^ me for k in range(per_row)]
    here = [row_ref[:, k : k + 1] == lane_block for k in range(per_row)]
    for j in range(groups):
        chosen = [jnp.where(here[k] & (slots[k] == j), 1, 0) for k in range(per_row)]
        placed = []
        for i in range(rows):
            x = jnp.zeros((width, wide), jnp.float32)
            for k in range(per_row):
                block = twice[i * per_row + k]
                x = jnp.where(chosen[k][i : i + 1] == 1, jnp.concatenate([block] * (rows // 2), axis=1), x)
            placed.append(x)
        b_hi, b_lo = split(jnp.concatenate(placed, axis=0))
        hi_ref[j], lo_ref[j] = split(dot3(rt_hi, rt_lo, b_hi, b_lo))


def spread(src, rows, width):
    lane = lax.broadcasted_iota(jnp.int32, (1, 2 * width), 1)
    low = jnp.where(lane < width, 0.0, 1.0)
    high = jnp.where(lane < width, 2.0, -1.0)
    base = rows * width
    near, far = [], []
    for s in range(rows):
        x = src[s * width : (s + 1) * width, :]
        y = pltpu.roll(x, width, 1)
        straight = src[base + s : base + s + 1, :]
        crossed = src[base + rows + s : base + rows + s + 1, :]
        near.append(jnp.where(straight == low, x, 0.0) + jnp.where(crossed == low, y, 0.0))
        far.append(jnp.where(straight == high, x, 0.0) + jnp.where(crossed == high, y, 0.0))
    return jnp.concatenate([jnp.concatenate(near, axis=0), jnp.concatenate(far, axis=0)], axis=1)


def multiply(hi_ref, lo_ref, slot, src, width):
    rows = hi_ref.shape[2] // width
    return dot3(hi_ref[slot], lo_ref[slot], *split(spread(src, rows, width)))


def lay_out(found, outs, width):
    swap = lax.axis_index("blk") % 2 == 1
    pair = 2 * width
    pairs = len(found) // 2
    right_half = lax.broadcasted_iota(jnp.int32, (width, pair), 1) >= width
    for q in range(pairs):
        for t, out_ref in enumerate(outs):
            a, b = (f[t * width : (t + 1) * width] for f in found[2 * q : 2 * q + 2])
            before = jnp.where(swap, b, a)
            after = jnp.where(swap, a, b)
            for e in range(SHIFTS):
                tile = slice((e // 2) * pair, (e // 2 + 1) * pair)
                u, v = before[:, tile], after[:, tile]
                if e % 2 == 0:
                    v = pltpu.roll(v, width, 1)
                else:
                    u = pltpu.roll(u, width, 1)
                at = (e * pairs + q) * pair
                out_ref[:, at : at + pair] = jnp.where(right_half, v, u)


def near_kernel(width, hi_ref, lo_ref, *refs):
    lay_out([multiply(hi_ref, lo_ref, j, src, width) for j, src in enumerate(refs[:-3])], refs[-3:], width)


def product_kernel(width, first, turn, earlier_ref, hi_ref, lo_ref, *refs):
    sources, out_ref = refs[:-1], refs[-1]

    @pl.when(lax.axis_index("band") % 2 == turn)
    def _():
        for j, src in enumerate(sources):
            out_ref[j] = multiply(hi_ref, lo_ref, first + j, src, width)


def join_kernel(width, turn, hi_ref, lo_ref, found_ref, last_ref, *refs):
    handed, outs = refs[:-3], refs[-3:]
    mine = lax.axis_index("band") % 2 == turn

    @pl.when(mine)
    def _():
        found = [found_ref[j] for j in range(found_ref.shape[0])]
        found.append(multiply(hi_ref, lo_ref, hi_ref.shape[0] - 1, last_ref, width))
        lay_out(found, outs, width)

    @pl.when(jnp.logical_not(mine))
    def _():
        for out_ref in outs[: 3 - len(handed)]:
            out_ref[...] = jnp.zeros_like(out_ref)
        for out_ref, given_ref in zip(outs[3 - len(handed) :], handed):
            out_ref[...] = given_ref[...]


def place(sum_ref, part_ref, groups, first, shift):
    me = lax.axis_index("blk")
    pair = 2 * part_ref.shape[0]
    pairs = part_ref.shape[1] // (SHIFTS * pair)
    for q in range(pairs):
        tile = (me ^ (first + 2 * q)) // 2
        for e in range(SHIFTS):
            at = pl.ds(pl.multiple_of(((e + shift) * (groups // 2) + tile) * pair, pair), pair)
            sum_ref[:, at] += part_ref[:, (e * pairs + q) * pair : (e * pairs + q + 1) * pair]


def first_kernel(groups, near_ref, far_ref, out_ref):
    out_ref[...] = jnp.zeros_like(out_ref)
    place(out_ref, near_ref, groups, 0, 1)
    place(out_ref, far_ref, groups, 0, 2 * (lax.axis_index("band") % 2))


def early_kernel(groups, first_ref, rest_ref, up_ref, out_ref):
    span = groups // 2
    out_ref[...] = first_ref[...]
    place(out_ref, rest_ref, groups, span, 1)
    place(out_ref, up_ref, groups, span * (1 - lax.axis_index("band") % 2), 0)


def late_kernel(groups, early_ref, down_ref, chip_ref, out_ref):
    odd = lax.axis_index("band") % 2
    span = groups // 2
    out_ref[...] = early_ref[...]
    place(out_ref, chip_ref, groups, span, 2 - 2 * odd)
    place(out_ref, down_ref, groups, span * odd, 2)


def body(fine_blocks, source_group, source_row, prolong_blocks, prolong_code):
    rows, width, pair = prolong_blocks.shape
    groups = lax.axis_size("blk")
    bands = lax.axis_size("band")
    f32 = jnp.float32
    prolong_code = prolong_code.T
    lanes = pl.pallas_call(
        lanes_kernel,
        out_shape=jax.ShapeDtypeStruct((1, pair), jnp.int32),
        out_specs=vmem(),
        cost_estimate=pl.CostEstimate(flops=4000000000, bytes_accessed=10000000, transcendentals=0),
        compiler_params=PARAMS,
        name="lanes",
    )()
    packed = pl.pallas_call(
        functools.partial(pack_kernel, width),
        out_shape=jax.ShapeDtypeStruct((rows * width + 2 * rows, pair), f32),
        in_specs=[vmem()] * 3,
        out_specs=vmem(),
        compiler_params=PARAMS,
        name="pack",
    )(lanes, prolong_code, prolong_blocks.reshape(rows * width, pair))
    height = SHIFTS * width
    deep = rows * width

    def call(kernel, name, shapes, dtype=f32, inputs=0, **more):
        more.setdefault("in_specs", [vmem()] * inputs)
        single = not isinstance(shapes, list)
        out = [jax.ShapeDtypeStruct(x, dtype) for x in ([shapes] if single else shapes)]
        return pl.pallas_call(
            kernel,
            out_shape=out[0] if single else out,
            out_specs=vmem() if single else [vmem()] * len(out),
            compiler_params=PARAMS,
            name=name,
            **more,
        )

    def gather(offsets):
        to = []
        for b in range(groups):
            for r in range(bands):
                offset = offsets[r % 2]
                other = (b, r ^ 2) if offset is None else (b ^ offset, r)
                to.append((b * bands + r, other[0] * bands + other[1]))
        return lax.ppermute(packed, ("blk", "band"), to)

    span = groups // 2
    sources = [packed] + [gather((j, j)) for j in range(1, span)]
    odd_steps = [*range(span, groups)] + [None] * LAG
    even_steps = [*range(span, groups - 1)] + [None] * LAG + [groups - 1]
    rest = [gather(offsets) for offsets in zip(even_steps, odd_steps)]
    hi, lo = pl.pallas_call(
        functools.partial(left_kernel, width),
        out_shape=[jax.ShapeDtypeStruct((groups, height, deep), jnp.bfloat16)] * 2,
        in_specs=[vmem()] * 5,
        out_specs=[vmem()] * 2,
        cost_estimate=pl.CostEstimate(
            flops=6 * groups * height * deep * deep, bytes_accessed=2000000, transcendentals=0
        ),
        compiler_params=PARAMS,
        name="left",
    )(source_group, source_row, prolong_code, fine_blocks, packed)

    def products(name, turn, sources, earlier):
        kernel = functools.partial(product_kernel, width, span, turn)
        specs = [pl.BlockSpec(memory_space=pl.ANY)] + [vmem()] * (2 + len(sources))
        shape = (len(sources), height, 2 * pair)
        return call(kernel, name, shape, in_specs=specs)(earlier, hi, lo, *sources)

    parts = [(width, SHIFTS * span * width)] * 3

    def join(name, turn, found, last, *handed):
        kernel = functools.partial(join_kernel, width, turn)
        return call(kernel, name, parts, inputs=4 + len(handed))(hi, lo, found, last, *handed)

    own_near, chip_near, far = call(
        functools.partial(near_kernel, width), "near", parts, inputs=2 + span
    )(hi, lo, *sources)
    far = lax.ppermute(far, "band", [(i, (i + 1 if i % 2 else i - 1) % bands) for i in range(bands)])
    found = products("rest_odd", 1, rest[: span - 1], own_near)
    own, chip, up = join("join_odd", 1, found, rest[span - 1], chip_near)
    up = lax.ppermute(up, "band", [(i, (i + 1) % bands) for i in range(bands)])
    found = products("rest_even", 0, rest[: span - 1], own)
    own, chip, down = join("join_even", 0, found, rest[-1], own, chip, chip_near)
    down = lax.ppermute(down, "band", [((i + 1) % bands, i) for i in range(bands)])
    chip = lax.ppermute(chip, "band", [(i, i ^ 1) for i in range(bands)])
    whole = (width, 5 * groups * width)
    slow = pl.CostEstimate(flops=4000000000, bytes_accessed=2000000, transcendentals=0)
    first = call(functools.partial(first_kernel, groups), "first", whole, inputs=2)(own_near, far)
    early = call(functools.partial(early_kernel, groups), "early", whole, inputs=3, cost_estimate=slow)(
        first, own, up
    )
    return call(functools.partial(late_kernel, groups), "late", whole, inputs=3)(early, down, chip)


def solution(mesh):
    return jax.shard_map(
        body,
        mesh=mesh,
        in_specs=(
            P(("blk", "band"), None, None),
            P(("blk", "band"), None),
            P(("blk", "band"), None),
            P(("blk", "band"), None, None),
            P(("blk", "band"), None),
        ),
        out_specs=P(("blk", "band"), None),
        check_vma=False,
    )
```

```python
import functools

import jax
import jax.numpy as jnp
from jax import lax
from jax.experimental import pallas as pl
from jax.experimental.pallas import tpu as pltpu
from jax.sharding import PartitionSpec as P

SHIFTS = 3
LAG = 1
PARAMS = pltpu.CompilerParams(vmem_limit_bytes=24 * 1024 * 1024)


def vmem():
    return pl.BlockSpec(memory_space=pltpu.VMEM)


def split(x):
    hi = x.astype(jnp.bfloat16)
    return hi, (x - hi.astype(jnp.float32)).astype(jnp.bfloat16)


def dot(a, b):
    return lax.dot_general(a, b, (((1,), (0,)), ((), ())), preferred_element_type=jnp.float32)


def dot3(a_hi, a_lo, b_hi, b_lo):
    return dot(a_hi, b_hi) + (dot(a_hi, b_lo) + dot(a_lo, b_hi))


def lanes_kernel(out_ref):
    pair = out_ref.shape[1]
    out_ref[...] = lax.broadcasted_iota(jnp.int32, out_ref.shape, 1) // (pair // 2)


def pack_kernel(width, lanes_ref, code_ref, p_ref, out_ref):
    deep = p_ref.shape[0]
    rows = deep // width
    out_ref[:deep, :] = p_ref[...]
    left = lanes_ref[...] == 0
    straight = [jnp.where(left, code_ref[0:1, i : i + 1], code_ref[1:2, i : i + 1]) for i in range(rows)]
    crossed = [jnp.where(left, code_ref[1:2, i : i + 1], code_ref[0:1, i : i + 1]) for i in range(rows)]
    out_ref[deep:, :] = jnp.concatenate(straight + crossed, axis=0).astype(jnp.float32)


def left_kernel(width, group_ref, row_ref, code_ref, a_ref, packed_ref, hi_ref, lo_ref):
    rows, per_row = group_ref.shape
    groups = hi_ref.shape[0]
    me = lax.axis_index("blk")
    odd = lax.axis_index("band") % 2
    pair = 2 * width
    wide = rows * width
    lane_block = lax.broadcasted_iota(jnp.int32, (rows, wide), 1) // width
    pt = packed_ref[:wide, :].T
    row_of = lane_block[:1]
    codes = []
    for n in range(2):
        c = jnp.broadcast_to(code_ref[n : n + 1, :1], (1, wide))
        for i in range(1, rows):
            c = jnp.where(row_of == i, code_ref[n : n + 1, i : i + 1], c)
        codes.append(c)
    blocks = []
    for dest in (1, 2 - 2 * odd, 2 * odd):
        blocks.append(
            jnp.where(codes[0] == dest, pt[:width], 0.0) + jnp.where(codes[1] == dest, pt[width:], 0.0)
        )
    rt_hi, rt_lo = split(jnp.concatenate(blocks, axis=0))
    left_half = lax.broadcasted_iota(jnp.int32, (width, pair), 1) < width
    twice = []
    for i in range(rows):
        for k in range(0, per_row, 2):
            x = a_ref[i, :, (k // 2) * pair : (k // 2 + 1) * pair]
            y = pltpu.roll(x, width, 1)
            twice += [jnp.where(left_half, x, y), jnp.where(left_half, y, x)]
    slots = [group_ref[:, k : k + 1] ^ me for k in range(per_row)]
    here = [row_ref[:, k : k + 1] == lane_block for k in range(per_row)]
    for j in range(groups):
        chosen = [jnp.where(here[k] & (slots[k] == j), 1, 0) for k in range(per_row)]
        placed = []
        for i in range(rows):
            x = jnp.zeros((width, wide), jnp.float32)
            for k in range(per_row):
                block = twice[i * per_row + k]
                x = jnp.where(chosen[k][i : i + 1] == 1, jnp.concatenate([block] * (rows // 2), axis=1), x)
            placed.append(x)
        b_hi, b_lo = split(jnp.concatenate(placed, axis=0))
        hi_ref[j], lo_ref[j] = split(dot3(rt_hi, rt_lo, b_hi, b_lo))


def spread(src, rows, width):
    lane = lax.broadcasted_iota(jnp.int32, (1, 2 * width), 1)
    low = jnp.where(lane < width, 0.0, 1.0)
    high = jnp.where(lane < width, 2.0, -1.0)
    base = rows * width
    near, far = [], []
    for s in range(rows):
        x = src[s * width : (s + 1) * width, :]
        y = pltpu.roll(x, width, 1)
        straight = src[base + s : base + s + 1, :]
        crossed = src[base + rows + s : base + rows + s + 1, :]
        near.append(jnp.where(straight == low, x, 0.0) + jnp.where(crossed == low, y, 0.0))
        far.append(jnp.where(straight == high, x, 0.0) + jnp.where(crossed == high, y, 0.0))
    return jnp.concatenate([jnp.concatenate(near, axis=0), jnp.concatenate(far, axis=0)], axis=1)


def multiply(hi_ref, lo_ref, slot, src, width):
    rows = hi_ref.shape[2] // width
    return dot3(hi_ref[slot], lo_ref[slot], *split(spread(src, rows, width)))


def lay_out(found, outs, width):
    swap = lax.axis_index("blk") % 2 == 1
    pair = 2 * width
    pairs = len(found) // 2
    right_half = lax.broadcasted_iota(jnp.int32, (width, pair), 1) >= width
    for q in range(pairs):
        for t, out_ref in enumerate(outs):
            a, b = (f[t * width : (t + 1) * width] for f in found[2 * q : 2 * q + 2])
            before = jnp.where(swap, b, a)
            after = jnp.where(swap, a, b)
            for e in range(SHIFTS):
                tile = slice((e // 2) * pair, (e // 2 + 1) * pair)
                u, v = before[:, tile], after[:, tile]
                if e % 2 == 0:
                    v = pltpu.roll(v, width, 1)
                else:
                    u = pltpu.roll(u, width, 1)
                at = (e * pairs + q) * pair
                out_ref[:, at : at + pair] = jnp.where(right_half, v, u)


def near_kernel(width, hi_ref, lo_ref, *refs):
    lay_out([multiply(hi_ref, lo_ref, j, src, width) for j, src in enumerate(refs[:-3])], refs[-3:], width)


def product_kernel(width, first, turn, earlier_ref, hi_ref, lo_ref, *refs):
    sources, out_ref = refs[:-1], refs[-1]

    @pl.when(lax.axis_index("band") % 2 == turn)
    def _():
        for j, src in enumerate(sources):
            out_ref[j] = multiply(hi_ref, lo_ref, first + j, src, width)


def join_kernel(width, turn, hi_ref, lo_ref, found_ref, last_ref, *refs):
    handed, outs = refs[:-3], refs[-3:]
    mine = lax.axis_index("band") % 2 == turn

    @pl.when(mine)
    def _():
        found = [found_ref[j] for j in range(found_ref.shape[0])]
        found.append(multiply(hi_ref, lo_ref, hi_ref.shape[0] - 1, last_ref, width))
        lay_out(found, outs, width)

    @pl.when(jnp.logical_not(mine))
    def _():
        for out_ref in outs[: 3 - len(handed)]:
            out_ref[...] = jnp.zeros_like(out_ref)
        for out_ref, given_ref in zip(outs[3 - len(handed) :], handed):
            out_ref[...] = given_ref[...]


def place(sum_ref, part_ref, groups, first, shift):
    me = lax.axis_index("blk")
    pair = 2 * part_ref.shape[0]
    pairs = part_ref.shape[1] // (SHIFTS * pair)
    for q in range(pairs):
        tile = (me ^ (first + 2 * q)) // 2
        for e in range(SHIFTS):
            at = pl.ds(pl.multiple_of(((e + shift) * (groups // 2) + tile) * pair, pair), pair)
            sum_ref[:, at] += part_ref[:, (e * pairs + q) * pair : (e * pairs + q + 1) * pair]


def first_kernel(groups, near_ref, far_ref, out_ref):
    out_ref[...] = jnp.zeros_like(out_ref)
    place(out_ref, near_ref, groups, 0, 1)
    place(out_ref, far_ref, groups, 0, 2 * (lax.axis_index("band") % 2))


def early_kernel(groups, first_ref, rest_ref, up_ref, out_ref):
    span = groups // 2
    out_ref[...] = first_ref[...]
    place(out_ref, rest_ref, groups, span, 1)
    place(out_ref, up_ref, groups, span * (1 - lax.axis_index("band") % 2), 0)


def late_kernel(groups, early_ref, down_ref, chip_ref, out_ref):
    odd = lax.axis_index("band") % 2
    span = groups // 2
    out_ref[...] = early_ref[...]
    place(out_ref, chip_ref, groups, span, 2 - 2 * odd)
    place(out_ref, down_ref, groups, span * odd, 2)


def body(fine_blocks, source_group, source_row, prolong_blocks, prolong_code):
    rows, width, pair = prolong_blocks.shape
    groups = lax.axis_size("blk")
    bands = lax.axis_size("band")
    f32 = jnp.float32
    prolong_code = prolong_code.T
    lanes = pl.pallas_call(
        lanes_kernel,
        out_shape=jax.ShapeDtypeStruct((1, pair), jnp.int32),
        out_specs=vmem(),
        cost_estimate=pl.CostEstimate(flops=4000000000, bytes_accessed=10000000, transcendentals=0),
        compiler_params=PARAMS,
        name="lanes",
    )()
    packed = pl.pallas_call(
        functools.partial(pack_kernel, width),
        out_shape=jax.ShapeDtypeStruct((rows * width + 2 * rows, pair), f32),
        in_specs=[vmem()] * 3,
        out_specs=vmem(),
        compiler_params=PARAMS,
        name="pack",
    )(lanes, prolong_code, prolong_blocks.reshape(rows * width, pair))
    height = SHIFTS * width
    deep = rows * width

    def call(kernel, name, shapes, dtype=f32, inputs=0, **more):
        more.setdefault("in_specs", [vmem()] * inputs)
        single = not isinstance(shapes, list)
        out = [jax.ShapeDtypeStruct(x, dtype) for x in ([shapes] if single else shapes)]
        return pl.pallas_call(
            kernel,
            out_shape=out[0] if single else out,
            out_specs=vmem() if single else [vmem()] * len(out),
            compiler_params=PARAMS,
            name=name,
            **more,
        )

    def idle(b, r):
        if r % 2:
            return b, r ^ 2
        if r == 0:
            return b ^ 1, r
        return b, r + 2 if r + 2 < bands else 2

    def gather(offsets):
        to = []
        for b in range(groups):
            for r in range(bands):
                offset = offsets[r % 2]
                other = idle(b, r) if offset is None else (b ^ offset, r)
                to.append((b * bands + r, other[0] * bands + other[1]))
        return lax.ppermute(packed, ("blk", "band"), to)

    span = groups // 2
    sources = [packed] + [gather((j, j)) for j in range(1, span)]
    odd_steps = [*range(span, groups)] + [None] * LAG
    even_steps = [*range(span, groups - 1)] + [None] * LAG + [groups - 1]
    rest = [gather(offsets) for offsets in zip(even_steps, odd_steps)]
    hi, lo = pl.pallas_call(
        functools.partial(left_kernel, width),
        out_shape=[jax.ShapeDtypeStruct((groups, height, deep), jnp.bfloat16)] * 2,
        in_specs=[vmem()] * 5,
        out_specs=[vmem()] * 2,
        cost_estimate=pl.CostEstimate(
            flops=6 * groups * height * deep * deep, bytes_accessed=2000000, transcendentals=0
        ),
        compiler_params=PARAMS,
        name="left",
    )(source_group, source_row, prolong_code, fine_blocks, packed)

    def products(name, turn, sources, earlier):
        kernel = functools.partial(product_kernel, width, span, turn)
        specs = [pl.BlockSpec(memory_space=pl.ANY)] + [vmem()] * (2 + len(sources))
        shape = (len(sources), height, 2 * pair)
        return call(kernel, name, shape, in_specs=specs)(earlier, hi, lo, *sources)

    parts = [(width, SHIFTS * span * width)] * 3

    def join(name, turn, found, last, *handed):
        kernel = functools.partial(join_kernel, width, turn)
        return call(kernel, name, parts, inputs=4 + len(handed))(hi, lo, found, last, *handed)

    own_near, chip_near, far = call(
        functools.partial(near_kernel, width), "near", parts, inputs=2 + span
    )(hi, lo, *sources)
    far = lax.ppermute(far, "band", [(i, (i + 1 if i % 2 else i - 1) % bands) for i in range(bands)])
    found = products("rest_odd", 1, rest[: span - 1], own_near)
    own, chip, up = join("join_odd", 1, found, rest[span - 1], chip_near)
    up = lax.ppermute(up, "band", [(i, (i + 1) % bands) for i in range(bands)])
    found = products("rest_even", 0, rest[: span - 1], own)
    own, chip, down = join("join_even", 0, found, rest[-1], own, chip, chip_near)
    down = lax.ppermute(down, "band", [((i + 1) % bands, i) for i in range(bands)])
    chip = lax.ppermute(chip, "band", [(i, i ^ 1) for i in range(bands)])
    whole = (width, 5 * groups * width)
    slow = pl.CostEstimate(flops=4000000000, bytes_accessed=2000000, transcendentals=0)
    first = call(functools.partial(first_kernel, groups), "first", whole, inputs=2)(own_near, far)
    early = call(functools.partial(early_kernel, groups), "early", whole, inputs=3, cost_estimate=slow)(
        first, own, up
    )
    return call(functools.partial(late_kernel, groups), "late", whole, inputs=3)(early, down, chip)


def solution(mesh):
    return jax.shard_map(
        body,
        mesh=mesh,
        in_specs=(
            P(("blk", "band"), None, None),
            P(("blk", "band"), None),
            P(("blk", "band"), None),
            P(("blk", "band"), None, None),
            P(("blk", "band"), None),
        ),
        out_specs=P(("blk", "band"), None),
        check_vma=False,
    )
```

```python
import functools

import jax
import jax.numpy as jnp
from jax import lax
from jax.experimental import pallas as pl
from jax.experimental.pallas import tpu as pltpu
from jax.sharding import PartitionSpec as P

SHIFTS = 3
LAG = 1
PARAMS = pltpu.CompilerParams(vmem_limit_bytes=24 * 1024 * 1024)


def vmem():
    return pl.BlockSpec(memory_space=pltpu.VMEM)


def split(x):
    hi = x.astype(jnp.bfloat16)
    return hi, (x - hi.astype(jnp.float32)).astype(jnp.bfloat16)


def dot(a, b):
    return lax.dot_general(a, b, (((1,), (0,)), ((), ())), preferred_element_type=jnp.float32)


def dot3(a_hi, a_lo, b_hi, b_lo):
    return dot(a_hi, b_hi) + (dot(a_hi, b_lo) + dot(a_lo, b_hi))


def lanes_kernel(out_ref):
    pair = out_ref.shape[1]
    out_ref[...] = lax.broadcasted_iota(jnp.int32, out_ref.shape, 1) // (pair // 2)


def pack_kernel(width, lanes_ref, code_ref, p_ref, out_ref):
    deep = p_ref.shape[0]
    rows = deep // width
    out_ref[:deep, :] = p_ref[...]
    left = lanes_ref[...] == 0
    straight = [jnp.where(left, code_ref[0:1, i : i + 1], code_ref[1:2, i : i + 1]) for i in range(rows)]
    crossed = [jnp.where(left, code_ref[1:2, i : i + 1], code_ref[0:1, i : i + 1]) for i in range(rows)]
    out_ref[deep:, :] = jnp.concatenate(straight + crossed, axis=0).astype(jnp.float32)


def left_kernel(width, group_ref, row_ref, code_ref, a_ref, packed_ref, hi_ref, lo_ref):
    rows, per_row = group_ref.shape
    groups = hi_ref.shape[0]
    me = lax.axis_index("blk")
    odd = lax.axis_index("band") % 2
    pair = 2 * width
    wide = rows * width
    lane_block = lax.broadcasted_iota(jnp.int32, (rows, wide), 1) // width
    pt = packed_ref[:wide, :].T
    row_of = lane_block[:1]
    codes = []
    for n in range(2):
        c = jnp.broadcast_to(code_ref[n : n + 1, :1], (1, wide))
        for i in range(1, rows):
            c = jnp.where(row_of == i, code_ref[n : n + 1, i : i + 1], c)
        codes.append(c)
    blocks = []
    for dest in (1, 2 - 2 * odd, 2 * odd):
        blocks.append(
            jnp.where(codes[0] == dest, pt[:width], 0.0) + jnp.where(codes[1] == dest, pt[width:], 0.0)
        )
    rt_hi, rt_lo = split(jnp.concatenate(blocks, axis=0))
    left_half = lax.broadcasted_iota(jnp.int32, (width, pair), 1) < width
    twice = []
    for i in range(rows):
        for k in range(0, per_row, 2):
            x = a_ref[i, :, (k // 2) * pair : (k // 2 + 1) * pair]
            y = pltpu.roll(x, width, 1)
            twice += [jnp.where(left_half, x, y), jnp.where(left_half, y, x)]
    slots = [group_ref[:, k : k + 1] ^ me for k in range(per_row)]
    here = [row_ref[:, k : k + 1] == lane_block for k in range(per_row)]
    for j in range(groups):
        chosen = [jnp.where(here[k] & (slots[k] == j), 1, 0) for k in range(per_row)]
        placed = []
        for i in range(rows):
            x = jnp.zeros((width, wide), jnp.float32)
            for k in range(per_row):
                block = twice[i * per_row + k]
                x = jnp.where(chosen[k][i : i + 1] == 1, jnp.concatenate([block] * (rows // 2), axis=1), x)
            placed.append(x)
        b_hi, b_lo = split(jnp.concatenate(placed, axis=0))
        hi_ref[j], lo_ref[j] = split(dot3(rt_hi, rt_lo, b_hi, b_lo))


def spread(src, rows, width):
    lane = lax.broadcasted_iota(jnp.int32, (1, 2 * width), 1)
    low = jnp.where(lane < width, 0.0, 1.0)
    high = jnp.where(lane < width, 2.0, -1.0)
    base = rows * width
    near, far = [], []
    for s in range(rows):
        x = src[s * width : (s + 1) * width, :]
        y = pltpu.roll(x, width, 1)
        straight = src[base + s : base + s + 1, :]
        crossed = src[base + rows + s : base + rows + s + 1, :]
        near.append(jnp.where(straight == low, x, 0.0) + jnp.where(crossed == low, y, 0.0))
        far.append(jnp.where(straight == high, x, 0.0) + jnp.where(crossed == high, y, 0.0))
    return jnp.concatenate([jnp.concatenate(near, axis=0), jnp.concatenate(far, axis=0)], axis=1)


def multiply(hi_ref, lo_ref, slot, src, width, at=slice(None)):
    rows = hi_ref.shape[2] // width
    return dot3(hi_ref[slot, at, :], lo_ref[slot, at, :], *split(spread(src, rows, width)))


def lay_out(found, outs, width):
    swap = lax.axis_index("blk") % 2 == 1
    pair = 2 * width
    pairs = len(found) // 2
    right_half = lax.broadcasted_iota(jnp.int32, (width, pair), 1) >= width
    for q in range(pairs):
        for t, out_ref in enumerate(outs):
            a, b = (f[t * width : (t + 1) * width] for f in found[2 * q : 2 * q + 2])
            before = jnp.where(swap, b, a)
            after = jnp.where(swap, a, b)
            for e in range(SHIFTS):
                tile = slice((e // 2) * pair, (e // 2 + 1) * pair)
                u, v = before[:, tile], after[:, tile]
                if e % 2 == 0:
                    v = pltpu.roll(v, width, 1)
                else:
                    u = pltpu.roll(u, width, 1)
                at = (e * pairs + q) * pair
                out_ref[:, at : at + pair] = jnp.where(right_half, v, u)


def near_kernel(width, hi_ref, lo_ref, *refs):
    lay_out([multiply(hi_ref, lo_ref, j, src, width) for j, src in enumerate(refs[:-3])], refs[-3:], width)


def product_kernel(width, first, turn, earlier_ref, hi_ref, lo_ref, *refs):
    sources, out_ref = refs[:-1], refs[-1]

    @pl.when(lax.axis_index("band") % 2 == turn)
    def _():
        for j, src in enumerate(sources):
            out_ref[j] = multiply(hi_ref, lo_ref, first + j, src, width)


def finish(width, at, hi_ref, lo_ref, found_ref, last_ref, outs):
    found = [found_ref[j, at, :] for j in range(found_ref.shape[0])]
    found.append(multiply(hi_ref, lo_ref, hi_ref.shape[0] - 1, last_ref, width, at))
    lay_out(found, outs, width)


def far_kernel(width, turn, hi_ref, lo_ref, found_ref, last_ref, given_ref, out_ref):
    mine = lax.axis_index("band") % 2 == turn

    @pl.when(mine)
    def _():
        finish(width, slice(2 * width, 3 * width), hi_ref, lo_ref, found_ref, last_ref, [out_ref])

    @pl.when(jnp.logical_not(mine))
    def _():
        out_ref[...] = given_ref[...]


def join_kernel(width, earlier_ref, hi_ref, lo_ref, *refs):
    outs = refs[-2:]
    odd = lax.axis_index("band") % 2 == 1
    at = slice(0, 2 * width)
    pl.when(odd)(lambda: finish(width, at, hi_ref, lo_ref, refs[0], refs[1], outs))
    pl.when(jnp.logical_not(odd))(lambda: finish(width, at, hi_ref, lo_ref, refs[2], refs[3], outs))


def place(sum_ref, part_ref, groups, first, shift):
    me = lax.axis_index("blk")
    pair = 2 * part_ref.shape[0]
    pairs = part_ref.shape[1] // (SHIFTS * pair)
    for q in range(pairs):
        tile = (me ^ (first + 2 * q)) // 2
        for e in range(SHIFTS):
            at = pl.ds(pl.multiple_of(((e + shift) * (groups // 2) + tile) * pair, pair), pair)
            sum_ref[:, at] += part_ref[:, (e * pairs + q) * pair : (e * pairs + q + 1) * pair]


def first_kernel(groups, near_ref, far_ref, out_ref):
    out_ref[...] = jnp.zeros_like(out_ref)
    place(out_ref, near_ref, groups, 0, 1)
    place(out_ref, far_ref, groups, 0, 2 * (lax.axis_index("band") % 2))


def early_kernel(groups, first_ref, rest_ref, up_ref, out_ref):
    span = groups // 2
    out_ref[...] = first_ref[...]
    place(out_ref, rest_ref, groups, span, 1)
    place(out_ref, up_ref, groups, span * (1 - lax.axis_index("band") % 2), 0)


def late_kernel(groups, early_ref, down_ref, chip_ref, out_ref):
    odd = lax.axis_index("band") % 2
    span = groups // 2
    out_ref[...] = early_ref[...]
    place(out_ref, chip_ref, groups, span, 2 - 2 * odd)
    place(out_ref, down_ref, groups, span * odd, 2)


def body(fine_blocks, source_group, source_row, prolong_blocks, prolong_code):
    rows, width, pair = prolong_blocks.shape
    groups = lax.axis_size("blk")
    bands = lax.axis_size("band")
    f32 = jnp.float32
    prolong_code = prolong_code.T
    lanes = pl.pallas_call(
        lanes_kernel,
        out_shape=jax.ShapeDtypeStruct((1, pair), jnp.int32),
        out_specs=vmem(),
        cost_estimate=pl.CostEstimate(flops=4000000000, bytes_accessed=10000000, transcendentals=0),
        compiler_params=PARAMS,
        name="lanes",
    )()
    packed = pl.pallas_call(
        functools.partial(pack_kernel, width),
        out_shape=jax.ShapeDtypeStruct((rows * width + 2 * rows, pair), f32),
        in_specs=[vmem()] * 3,
        out_specs=vmem(),
        compiler_params=PARAMS,
        name="pack",
    )(lanes, prolong_code, prolong_blocks.reshape(rows * width, pair))
    height = SHIFTS * width
    deep = rows * width

    def call(kernel, name, shapes, dtype=f32, inputs=0, **more):
        more.setdefault("in_specs", [vmem()] * inputs)
        single = not isinstance(shapes, list)
        out = [jax.ShapeDtypeStruct(x, dtype) for x in ([shapes] if single else shapes)]
        return pl.pallas_call(
            kernel,
            out_shape=out[0] if single else out,
            out_specs=vmem() if single else [vmem()] * len(out),
            compiler_params=PARAMS,
            name=name,
            **more,
        )

    def idle(b, r):
        if r % 2:
            return b, (r + 2) % bands
        if r == 0:
            return b ^ 1, r
        return b, r + 2 if r + 2 < bands else 2

    def gather(offsets):
        to = []
        for b in range(groups):
            for r in range(bands):
                offset = offsets[r % 2]
                other = idle(b, r) if offset is None else (b ^ offset, r)
                to.append((b * bands + r, other[0] * bands + other[1]))
        return lax.ppermute(packed, ("blk", "band"), to)

    span = groups // 2
    sources = [packed] + [gather((j, j)) for j in range(1, span)]
    odd_steps = [*range(span, groups)] + [None] * LAG
    even_steps = [*range(span, groups - 1)] + [None] * LAG + [groups - 1]
    rest = [gather(offsets) for offsets in zip(even_steps, odd_steps)]
    hi, lo = pl.pallas_call(
        functools.partial(left_kernel, width),
        out_shape=[jax.ShapeDtypeStruct((groups, height, deep), jnp.bfloat16)] * 2,
        in_specs=[vmem()] * 5,
        out_specs=[vmem()] * 2,
        cost_estimate=pl.CostEstimate(
            flops=6 * groups * height * deep * deep, bytes_accessed=2000000, transcendentals=0
        ),
        compiler_params=PARAMS,
        name="left",
    )(source_group, source_row, prolong_code, fine_blocks, packed)

    def products(name, turn, sources, earlier):
        kernel = functools.partial(product_kernel, width, span, turn)
        specs = [pl.BlockSpec(memory_space=pl.ANY)] + [vmem()] * (2 + len(sources))
        shape = (len(sources), height, 2 * pair)
        return call(kernel, name, shape, in_specs=specs)(earlier, hi, lo, *sources)

    parts = [(width, SHIFTS * span * width)] * 3

    def far_part(name, turn, found, last):
        kernel = functools.partial(far_kernel, width, turn)
        return call(kernel, name, parts[0], inputs=5)(hi, lo, found, last, chip_near)

    own_near, chip_near, far = call(
        functools.partial(near_kernel, width), "near", parts, inputs=2 + span
    )(hi, lo, *sources)
    far = lax.ppermute(far, "band", [(i, (i + 1 if i % 2 else i - 1) % bands) for i in range(bands)])
    odd_found = products("rest_odd", 1, rest[: span - 1], own_near)
    far_up = far_part("far_odd", 1, odd_found, rest[span - 1])
    up = lax.ppermute(far_up, "band", [(i, (i + 1) % bands) for i in range(bands)])
    even_found = products("rest_even", 0, rest[: span - 1], far_up)
    far_down = far_part("far_even", 0, even_found, rest[-1])
    down = lax.ppermute(far_down, "band", [((i + 1) % bands, i) for i in range(bands)])
    own, chip = call(
        functools.partial(join_kernel, width),
        "join",
        parts[:2],
        in_specs=[pl.BlockSpec(memory_space=pl.ANY)] + [vmem()] * 6,
    )(far_down, hi, lo, odd_found, rest[span - 1], even_found, rest[-1])
    chip = lax.ppermute(chip, "band", [(i, i ^ 1) for i in range(bands)])
    whole = (width, 5 * groups * width)
    slow = pl.CostEstimate(flops=4000000000, bytes_accessed=2000000, transcendentals=0)
    first = call(functools.partial(first_kernel, groups), "first", whole, inputs=2)(own_near, far)
    early = call(functools.partial(early_kernel, groups), "early", whole, inputs=3, cost_estimate=slow)(
        first, own, up
    )
    return call(functools.partial(late_kernel, groups), "late", whole, inputs=3)(early, down, chip)


def solution(mesh):
    return jax.shard_map(
        body,
        mesh=mesh,
        in_specs=(
            P(("blk", "band"), None, None),
            P(("blk", "band"), None),
            P(("blk", "band"), None),
            P(("blk", "band"), None, None),
            P(("blk", "band"), None),
        ),
        out_specs=P(("blk", "band"), None),
        check_vma=False,
    )
```

```python
import functools

import jax
import jax.numpy as jnp
from jax import lax
from jax.experimental import pallas as pl
from jax.experimental.pallas import tpu as pltpu
from jax.sharding import PartitionSpec as P

SHIFTS = 3
LAG = 1
PARAMS = pltpu.CompilerParams(vmem_limit_bytes=24 * 1024 * 1024)


def vmem():
    return pl.BlockSpec(memory_space=pltpu.VMEM)


def split(x):
    hi = x.astype(jnp.bfloat16)
    return hi, (x - hi.astype(jnp.float32)).astype(jnp.bfloat16)


def dot(a, b):
    return lax.dot_general(a, b, (((1,), (0,)), ((), ())), preferred_element_type=jnp.float32)


def dot3(a_hi, a_lo, b_hi, b_lo):
    return dot(a_hi, b_hi) + (dot(a_hi, b_lo) + dot(a_lo, b_hi))


def lanes_kernel(out_ref):
    pair = out_ref.shape[1]
    out_ref[...] = lax.broadcasted_iota(jnp.int32, out_ref.shape, 1) // (pair // 2)


def pack_kernel(width, lanes_ref, code_ref, p_ref, out_ref):
    deep = p_ref.shape[0]
    rows = deep // width
    out_ref[:deep, :] = p_ref[...]
    left = lanes_ref[...] == 0
    straight = [jnp.where(left, code_ref[0:1, i : i + 1], code_ref[1:2, i : i + 1]) for i in range(rows)]
    crossed = [jnp.where(left, code_ref[1:2, i : i + 1], code_ref[0:1, i : i + 1]) for i in range(rows)]
    out_ref[deep:, :] = jnp.concatenate(straight + crossed, axis=0).astype(jnp.float32)


def left_kernel(width, group_ref, row_ref, code_ref, a_ref, packed_ref, hi_ref, lo_ref, far_ref):
    rows, per_row = group_ref.shape
    groups = hi_ref.shape[0]
    me = lax.axis_index("blk")
    odd = lax.axis_index("band") % 2
    pair = 2 * width
    wide = rows * width
    lane_block = lax.broadcasted_iota(jnp.int32, (rows, wide), 1) // width
    pt = packed_ref[:wide, :].T
    row_of = lane_block[:1]
    codes = []
    for n in range(2):
        c = jnp.broadcast_to(code_ref[n : n + 1, :1], (1, wide))
        for i in range(1, rows):
            c = jnp.where(row_of == i, code_ref[n : n + 1, i : i + 1], c)
        codes.append(c)
    blocks = []
    for dest in (1, 2 - 2 * odd, 2 * odd):
        blocks.append(
            jnp.where(codes[0] == dest, pt[:width], 0.0) + jnp.where(codes[1] == dest, pt[width:], 0.0)
        )
    rt_hi, rt_lo = split(jnp.concatenate(blocks, axis=0))
    left_half = lax.broadcasted_iota(jnp.int32, (width, pair), 1) < width
    twice = []
    for i in range(rows):
        for k in range(0, per_row, 2):
            x = a_ref[i, :, (k // 2) * pair : (k // 2 + 1) * pair]
            y = pltpu.roll(x, width, 1)
            twice += [jnp.where(left_half, x, y), jnp.where(left_half, y, x)]
    slots = [group_ref[:, k : k + 1] ^ me for k in range(per_row)]
    here = [row_ref[:, k : k + 1] == lane_block for k in range(per_row)]
    for j in range(groups):
        chosen = [jnp.where(here[k] & (slots[k] == j), 1, 0) for k in range(per_row)]
        placed = []
        for i in range(rows):
            x = jnp.zeros((width, wide), jnp.float32)
            for k in range(per_row):
                block = twice[i * per_row + k]
                x = jnp.where(chosen[k][i : i + 1] == 1, jnp.concatenate([block] * (rows // 2), axis=1), x)
            placed.append(x)
        b_hi, b_lo = split(jnp.concatenate(placed, axis=0))
        hi_ref[j], lo_ref[j] = split(dot3(rt_hi, rt_lo, b_hi, b_lo))
    far_ref[...] = multiply(hi_ref, lo_ref, 0, packed_ref, width, slice(2 * width, 3 * width))


def spread(src, rows, width):
    lane = lax.broadcasted_iota(jnp.int32, (1, 2 * width), 1)
    low = jnp.where(lane < width, 0.0, 1.0)
    high = jnp.where(lane < width, 2.0, -1.0)
    base = rows * width
    near, far = [], []
    for s in range(rows):
        x = src[s * width : (s + 1) * width, :]
        y = pltpu.roll(x, width, 1)
        straight = src[base + s : base + s + 1, :]
        crossed = src[base + rows + s : base + rows + s + 1, :]
        near.append(jnp.where(straight == low, x, 0.0) + jnp.where(crossed == low, y, 0.0))
        far.append(jnp.where(straight == high, x, 0.0) + jnp.where(crossed == high, y, 0.0))
    return jnp.concatenate([jnp.concatenate(near, axis=0), jnp.concatenate(far, axis=0)], axis=1)


def multiply(hi_ref, lo_ref, slot, src, width, at=slice(None)):
    rows = hi_ref.shape[2] // width
    return dot3(hi_ref[slot, at, :], lo_ref[slot, at, :], *split(spread(src, rows, width)))


def lay_out(found, outs, width):
    swap = lax.axis_index("blk") % 2 == 1
    pair = 2 * width
    pairs = len(found) // 2
    right_half = lax.broadcasted_iota(jnp.int32, (width, pair), 1) >= width
    for q in range(pairs):
        for t, out_ref in enumerate(outs):
            a, b = (f[t * width : (t + 1) * width] for f in found[2 * q : 2 * q + 2])
            before = jnp.where(swap, b, a)
            after = jnp.where(swap, a, b)
            for e in range(SHIFTS):
                tile = slice((e // 2) * pair, (e // 2 + 1) * pair)
                u, v = before[:, tile], after[:, tile]
                if e % 2 == 0:
                    v = pltpu.roll(v, width, 1)
                else:
                    u = pltpu.roll(u, width, 1)
                at = (e * pairs + q) * pair
                out_ref[:, at : at + pair] = jnp.where(right_half, v, u)


def near_kernel(width, hi_ref, lo_ref, own_ref, *refs):
    at = slice(2 * width, 3 * width)
    found = [multiply(hi_ref, lo_ref, 1 + j, src, width, at) for j, src in enumerate(refs[:-1])]
    lay_out([own_ref[...]] + found, refs[-1:], width)


def product_kernel(width, first, turn, earlier_ref, hi_ref, lo_ref, *refs):
    sources, out_ref = refs[:-1], refs[-1]

    @pl.when(lax.axis_index("band") % 2 == turn)
    def _():
        for j, src in enumerate(sources):
            out_ref[j] = multiply(hi_ref, lo_ref, first + j, src, width)


def finish(width, at, hi_ref, lo_ref, found_ref, last_ref, outs):
    found = [found_ref[j, at, :] for j in range(found_ref.shape[0])]
    found.append(multiply(hi_ref, lo_ref, hi_ref.shape[0] - 1, last_ref, width, at))
    lay_out(found, outs, width)


def far_kernel(width, turn, hi_ref, lo_ref, found_ref, last_ref, out_ref):
    mine = lax.axis_index("band") % 2 == turn

    @pl.when(mine)
    def _():
        finish(width, slice(2 * width, 3 * width), hi_ref, lo_ref, found_ref, last_ref, [out_ref])

    @pl.when(jnp.logical_not(mine))
    def _():
        out_ref[...] = jnp.zeros_like(out_ref)


def join_kernel(width, earlier_ref, hi_ref, lo_ref, *refs):
    sources, (near_ref, rest_ref, chip_ref) = refs[4:-3], refs[-3:]
    odd = lax.axis_index("band") % 2 == 1
    at = slice(0, 2 * width)
    found = [multiply(hi_ref, lo_ref, j, src, width, at) for j, src in enumerate(sources)]
    lay_out(found, [near_ref, chip_ref.at[:width]], width)
    outs = [rest_ref, chip_ref.at[width:]]
    pl.when(odd)(lambda: finish(width, at, hi_ref, lo_ref, refs[0], refs[1], outs))
    pl.when(jnp.logical_not(odd))(lambda: finish(width, at, hi_ref, lo_ref, refs[2], refs[3], outs))


def place(sum_ref, part_ref, groups, first, shift):
    me = lax.axis_index("blk")
    pair = 2 * part_ref.shape[0]
    pairs = part_ref.shape[1] // (SHIFTS * pair)
    for q in range(pairs):
        tile = (me ^ (first + 2 * q)) // 2
        for e in range(SHIFTS):
            at = pl.ds(pl.multiple_of(((e + shift) * (groups // 2) + tile) * pair, pair), pair)
            sum_ref[:, at] += part_ref[:, (e * pairs + q) * pair : (e * pairs + q + 1) * pair]


def first_kernel(groups, near_ref, far_ref, out_ref):
    out_ref[...] = jnp.zeros_like(out_ref)
    place(out_ref, near_ref, groups, 0, 1)
    place(out_ref, far_ref, groups, 0, 2 * (lax.axis_index("band") % 2))


def early_kernel(groups, first_ref, rest_ref, up_ref, out_ref):
    span = groups // 2
    out_ref[...] = first_ref[...]
    place(out_ref, rest_ref, groups, span, 1)
    place(out_ref, up_ref, groups, span, 0)


def late_kernel(groups, early_ref, down_ref, chip_ref, out_ref):
    odd = lax.axis_index("band") % 2
    span = groups // 2
    height = early_ref.shape[0]
    out_ref[...] = early_ref[...]
    place(out_ref, chip_ref.at[:height], groups, 0, 2 - 2 * odd)
    place(out_ref, chip_ref.at[height:], groups, span, 2 - 2 * odd)
    place(out_ref, down_ref, groups, span, 2)


def body(fine_blocks, source_group, source_row, prolong_blocks, prolong_code):
    rows, width, pair = prolong_blocks.shape
    groups = lax.axis_size("blk")
    bands = lax.axis_size("band")
    f32 = jnp.float32
    prolong_code = prolong_code.T
    lanes = pl.pallas_call(
        lanes_kernel,
        out_shape=jax.ShapeDtypeStruct((1, pair), jnp.int32),
        out_specs=vmem(),
        cost_estimate=pl.CostEstimate(flops=4000000000, bytes_accessed=10000000, transcendentals=0),
        compiler_params=PARAMS,
        name="lanes",
    )()
    packed = pl.pallas_call(
        functools.partial(pack_kernel, width),
        out_shape=jax.ShapeDtypeStruct((rows * width + 2 * rows, pair), f32),
        in_specs=[vmem()] * 3,
        out_specs=vmem(),
        compiler_params=PARAMS,
        name="pack",
    )(lanes, prolong_code, prolong_blocks.reshape(rows * width, pair))
    height = SHIFTS * width
    deep = rows * width

    def call(kernel, name, shapes, dtype=f32, inputs=0, **more):
        more.setdefault("in_specs", [vmem()] * inputs)
        single = not isinstance(shapes, list)
        out = [jax.ShapeDtypeStruct(x, dtype) for x in ([shapes] if single else shapes)]
        return pl.pallas_call(
            kernel,
            out_shape=out[0] if single else out,
            out_specs=vmem() if single else [vmem()] * len(out),
            compiler_params=PARAMS,
            name=name,
            **more,
        )

    def idle(b, r):
        if r % 2:
            return b, (r + 2) % bands
        if r == 0:
            return b ^ 1, r
        return b, r + 2 if r + 2 < bands else 2

    def gather(offsets):
        to = []
        for b in range(groups):
            for r in range(bands):
                offset = offsets[r % 2]
                other = idle(b, r) if offset is None else (b ^ offset, r)
                to.append((b * bands + r, other[0] * bands + other[1]))
        return lax.ppermute(packed, ("blk", "band"), to)

    span = groups // 2
    sources = [packed] + [gather((j, j)) for j in range(1, span)]
    odd_steps = [*range(span, groups)] + [None] * LAG
    even_steps = [*range(span, groups - 1)] + [None] * LAG + [groups - 1]
    rest = [gather(offsets) for offsets in zip(even_steps, odd_steps)]
    hi, lo, own_far = pl.pallas_call(
        functools.partial(left_kernel, width),
        out_shape=[jax.ShapeDtypeStruct((groups, height, deep), jnp.bfloat16)] * 2
        + [jax.ShapeDtypeStruct((width, 2 * pair), f32)],
        in_specs=[vmem()] * 5,
        out_specs=[vmem()] * 3,
        cost_estimate=pl.CostEstimate(
            flops=6 * groups * height * deep * deep, bytes_accessed=2000000, transcendentals=0
        ),
        compiler_params=PARAMS,
        name="left",
    )(source_group, source_row, prolong_code, fine_blocks, packed)

    def products(name, turn, sources, earlier):
        kernel = functools.partial(product_kernel, width, span, turn)
        specs = [pl.BlockSpec(memory_space=pl.ANY)] + [vmem()] * (2 + len(sources))
        shape = (len(sources), height, 2 * pair)
        return call(kernel, name, shape, in_specs=specs)(earlier, hi, lo, *sources)

    parts = [(width, SHIFTS * span * width)] * 3

    def far_part(name, turn, found, last):
        kernel = functools.partial(far_kernel, width, turn)
        return call(kernel, name, parts[0], inputs=4)(hi, lo, found, last)

    far_near = call(functools.partial(near_kernel, width), "near", parts[0], inputs=2 + span)(
        hi, lo, own_far, *sources[1:]
    )
    far = lax.ppermute(far_near, "band", [(i, (i + 1 if i % 2 else i - 1) % bands) for i in range(bands)])
    odd_found = products("rest_odd", 1, rest[: span - 1], far_near)
    far_up = far_part("far_odd", 1, odd_found, rest[span - 1])
    up = lax.ppermute(far_up, "band", [(i, (i + 1) % bands) for i in range(bands)])
    even_found = products("rest_even", 0, rest[: span - 1], far_up)
    far_down = far_part("far_even", 0, even_found, rest[-1])
    down = lax.ppermute(far_down, "band", [((i + 1) % bands, i) for i in range(bands)])
    own_near, own, chip = call(
        functools.partial(join_kernel, width),
        "join",
        [parts[0], parts[0], (2 * width, parts[0][1])],
        in_specs=[pl.BlockSpec(memory_space=pl.ANY)] + [vmem()] * (6 + span),
    )(far_down, hi, lo, odd_found, rest[span - 1], even_found, rest[-1], *sources)
    chip = lax.ppermute(chip, "band", [(i, i ^ 1) for i in range(bands)])
    whole = (width, 5 * groups * width)
    slow = pl.CostEstimate(flops=4000000000, bytes_accessed=2000000, transcendentals=0)
    first = call(functools.partial(first_kernel, groups), "first", whole, inputs=2)(own_near, far)
    early = call(functools.partial(early_kernel, groups), "early", whole, inputs=3, cost_estimate=slow)(
        first, own, up
    )
    return call(functools.partial(late_kernel, groups), "late", whole, inputs=3)(early, down, chip)


def solution(mesh):
    return jax.shard_map(
        body,
        mesh=mesh,
        in_specs=(
            P(("blk", "band"), None, None),
            P(("blk", "band"), None),
            P(("blk", "band"), None),
            P(("blk", "band"), None, None),
            P(("blk", "band"), None),
        ),
        out_specs=P(("blk", "band"), None),
        check_vma=False,
    )
```

```python
import functools

import jax
import jax.numpy as jnp
from jax import lax
from jax.experimental import pallas as pl
from jax.experimental.pallas import tpu as pltpu
from jax.sharding import PartitionSpec as P

SHIFTS = 3
LAG = 1
PARAMS = pltpu.CompilerParams(vmem_limit_bytes=24 * 1024 * 1024)


def vmem():
    return pl.BlockSpec(memory_space=pltpu.VMEM)


def split(x):
    hi = x.astype(jnp.bfloat16)
    return hi, (x - hi.astype(jnp.float32)).astype(jnp.bfloat16)


def dot(a, b):
    return lax.dot_general(a, b, (((1,), (0,)), ((), ())), preferred_element_type=jnp.float32)


def dot3(a_hi, a_lo, b_hi, b_lo):
    return dot(a_hi, b_hi) + (dot(a_hi, b_lo) + dot(a_lo, b_hi))


def lanes_kernel(out_ref):
    pair = out_ref.shape[1]
    out_ref[...] = lax.broadcasted_iota(jnp.int32, out_ref.shape, 1) // (pair // 2)


def pack_kernel(width, lanes_ref, code_ref, p_ref, out_ref):
    deep = p_ref.shape[0]
    rows = deep // width
    out_ref[:deep, :] = p_ref[...]
    left = lanes_ref[...] == 0
    straight = [jnp.where(left, code_ref[0:1, i : i + 1], code_ref[1:2, i : i + 1]) for i in range(rows)]
    crossed = [jnp.where(left, code_ref[1:2, i : i + 1], code_ref[0:1, i : i + 1]) for i in range(rows)]
    out_ref[deep:, :] = jnp.concatenate(straight + crossed, axis=0).astype(jnp.float32)


def left_kernel(width, group_ref, row_ref, code_ref, a_ref, packed_ref, hi_ref, lo_ref, far_ref):
    rows, per_row = group_ref.shape
    groups = hi_ref.shape[0]
    me = lax.axis_index("blk")
    odd = lax.axis_index("band") % 2
    pair = 2 * width
    wide = rows * width
    lane_block = lax.broadcasted_iota(jnp.int32, (rows, wide), 1) // width
    pt = packed_ref[:wide, :].T
    row_of = lane_block[:1]
    codes = []
    for n in range(2):
        c = jnp.broadcast_to(code_ref[n : n + 1, :1], (1, wide))
        for i in range(1, rows):
            c = jnp.where(row_of == i, code_ref[n : n + 1, i : i + 1], c)
        codes.append(c)
    blocks = []
    for dest in (1, 2 - 2 * odd, 2 * odd):
        blocks.append(
            jnp.where(codes[0] == dest, pt[:width], 0.0) + jnp.where(codes[1] == dest, pt[width:], 0.0)
        )
    rt_hi, rt_lo = split(jnp.concatenate(blocks, axis=0))
    left_half = lax.broadcasted_iota(jnp.int32, (width, pair), 1) < width
    twice = []
    for i in range(rows):
        for k in range(0, per_row, 2):
            x = a_ref[i, :, (k // 2) * pair : (k // 2 + 1) * pair]
            y = pltpu.roll(x, width, 1)
            twice += [jnp.where(left_half, x, y), jnp.where(left_half, y, x)]
    slots = [group_ref[:, k : k + 1] ^ me for k in range(per_row)]
    here = [row_ref[:, k : k + 1] == lane_block for k in range(per_row)]
    for j in range(groups):
        chosen = [jnp.where(here[k] & (slots[k] == j), 1, 0) for k in range(per_row)]
        placed = []
        for i in range(rows):
            x = jnp.zeros((width, wide), jnp.float32)
            for k in range(per_row):
                block = twice[i * per_row + k]
                x = jnp.where(chosen[k][i : i + 1] == 1, jnp.concatenate([block] * (rows // 2), axis=1), x)
            placed.append(x)
        b_hi, b_lo = split(jnp.concatenate(placed, axis=0))
        hi_ref[j], lo_ref[j] = split(dot3(rt_hi, rt_lo, b_hi, b_lo))
    far_ref[...] = multiply(hi_ref, lo_ref, 0, packed_ref, width, slice(2 * width, 3 * width))


def spread(src, rows, width):
    lane = lax.broadcasted_iota(jnp.int32, (1, 2 * width), 1)
    low = jnp.where(lane < width, 0.0, 1.0)
    high = jnp.where(lane < width, 2.0, -1.0)
    base = rows * width
    near, far = [], []
    for s in range(rows):
        x = src[s * width : (s + 1) * width, :]
        y = pltpu.roll(x, width, 1)
        straight = src[base + s : base + s + 1, :]
        crossed = src[base + rows + s : base + rows + s + 1, :]
        near.append(jnp.where(straight == low, x, 0.0) + jnp.where(crossed == low, y, 0.0))
        far.append(jnp.where(straight == high, x, 0.0) + jnp.where(crossed == high, y, 0.0))
    return jnp.concatenate([jnp.concatenate(near, axis=0), jnp.concatenate(far, axis=0)], axis=1)


def multiply(hi_ref, lo_ref, slot, src, width, at=slice(None)):
    rows = hi_ref.shape[2] // width
    return dot3(hi_ref[slot, at, :], lo_ref[slot, at, :], *split(spread(src, rows, width)))


def lay_out(found, outs, width):
    swap = lax.axis_index("blk") % 2 == 1
    pair = 2 * width
    pairs = len(found) // 2
    right_half = lax.broadcasted_iota(jnp.int32, (width, pair), 1) >= width
    for q in range(pairs):
        for t, out_ref in enumerate(outs):
            a, b = (f[t * width : (t + 1) * width] for f in found[2 * q : 2 * q + 2])
            before = jnp.where(swap, b, a)
            after = jnp.where(swap, a, b)
            for e in range(SHIFTS):
                tile = slice((e // 2) * pair, (e // 2 + 1) * pair)
                u, v = before[:, tile], after[:, tile]
                if e % 2 == 0:
                    v = pltpu.roll(v, width, 1)
                else:
                    u = pltpu.roll(u, width, 1)
                at = (e * pairs + q) * pair
                out_ref[:, at : at + pair] = jnp.where(right_half, v, u)


def near_kernel(width, hi_ref, lo_ref, own_ref, *refs):
    at = slice(2 * width, 3 * width)
    found = [multiply(hi_ref, lo_ref, 1 + j, src, width, at) for j, src in enumerate(refs[:-1])]
    lay_out([own_ref[...]] + found, refs[-1:], width)


def product_kernel(width, first, turn, earlier_ref, hi_ref, lo_ref, *refs):
    sources, out_ref = refs[:-1], refs[-1]

    @pl.when(lax.axis_index("band") % 2 == turn)
    def _():
        for j, src in enumerate(sources):
            out_ref[j] = multiply(hi_ref, lo_ref, first + j, src, width)


def finish(width, at, hi_ref, lo_ref, found_ref, last_ref, outs):
    found = [found_ref[j, at, :] for j in range(found_ref.shape[0])]
    found.append(multiply(hi_ref, lo_ref, hi_ref.shape[0] - 1, last_ref, width, at))
    lay_out(found, outs, width)


def far_kernel(width, turn, hi_ref, lo_ref, found_ref, last_ref, out_ref):
    mine = lax.axis_index("band") % 2 == turn

    @pl.when(mine)
    def _():
        finish(width, slice(2 * width, 3 * width), hi_ref, lo_ref, found_ref, last_ref, [out_ref])

    @pl.when(jnp.logical_not(mine))
    def _():
        out_ref[...] = jnp.zeros_like(out_ref)


def join_kernel(width, earlier_ref, hi_ref, lo_ref, *refs):
    sources, (near_ref, rest_ref, chip_ref) = refs[4:-3], refs[-3:]
    odd = lax.axis_index("band") % 2 == 1
    at = slice(0, 2 * width)
    found = [multiply(hi_ref, lo_ref, j, src, width, at) for j, src in enumerate(sources)]
    lay_out(found, [near_ref, chip_ref.at[:width]], width)
    outs = [rest_ref, chip_ref.at[width:]]
    pl.when(odd)(lambda: finish(width, at, hi_ref, lo_ref, refs[0], refs[1], outs))
    pl.when(jnp.logical_not(odd))(lambda: finish(width, at, hi_ref, lo_ref, refs[2], refs[3], outs))


def place(sum_ref, part_ref, groups, first, shift):
    me = lax.axis_index("blk")
    pair = 2 * part_ref.shape[0]
    pairs = part_ref.shape[1] // (SHIFTS * pair)
    for q in range(pairs):
        tile = (me ^ (first + 2 * q)) // 2
        for e in range(SHIFTS):
            at = pl.ds(pl.multiple_of(((e + shift) * (groups // 2) + tile) * pair, pair), pair)
            sum_ref[:, at] += part_ref[:, (e * pairs + q) * pair : (e * pairs + q + 1) * pair]


def first_kernel(groups, near_ref, far_ref, out_ref):
    out_ref[...] = jnp.zeros_like(out_ref)
    place(out_ref, near_ref, groups, 0, 1)
    place(out_ref, far_ref, groups, 0, 2 * (lax.axis_index("band") % 2))


def early_kernel(groups, first_ref, rest_ref, up_ref, out_ref):
    span = groups // 2
    out_ref[...] = first_ref[...]
    place(out_ref, rest_ref, groups, span, 1)
    place(out_ref, up_ref, groups, span, 0)


def late_kernel(groups, early_ref, down_ref, chip_ref, out_ref):
    odd = lax.axis_index("band") % 2
    span = groups // 2
    height = early_ref.shape[0]
    out_ref[...] = early_ref[...]
    place(out_ref, chip_ref.at[:height], groups, 0, 2 - 2 * odd)
    place(out_ref, chip_ref.at[height:], groups, span, 2 - 2 * odd)
    place(out_ref, down_ref, groups, span, 2)


def body(fine_blocks, source_group, source_row, prolong_blocks, prolong_code):
    rows, width, pair = prolong_blocks.shape
    groups = lax.axis_size("blk")
    bands = lax.axis_size("band")
    f32 = jnp.float32
    prolong_code = prolong_code.T
    lanes = pl.pallas_call(
        lanes_kernel,
        out_shape=jax.ShapeDtypeStruct((1, pair), jnp.int32),
        out_specs=vmem(),
        cost_estimate=pl.CostEstimate(flops=4000000000, bytes_accessed=10000000, transcendentals=0),
        compiler_params=PARAMS,
        name="lanes",
    )()
    packed = pl.pallas_call(
        functools.partial(pack_kernel, width),
        out_shape=jax.ShapeDtypeStruct((rows * width + 2 * rows, pair), f32),
        in_specs=[vmem()] * 3,
        out_specs=vmem(),
        compiler_params=PARAMS,
        name="pack",
    )(lanes, prolong_code, prolong_blocks.reshape(rows * width, pair))
    height = SHIFTS * width
    deep = rows * width

    def call(kernel, name, shapes, dtype=f32, inputs=0, **more):
        more.setdefault("in_specs", [vmem()] * inputs)
        single = not isinstance(shapes, list)
        out = [jax.ShapeDtypeStruct(x, dtype) for x in ([shapes] if single else shapes)]
        return pl.pallas_call(
            kernel,
            out_shape=out[0] if single else out,
            out_specs=vmem() if single else [vmem()] * len(out),
            compiler_params=PARAMS,
            name=name,
            **more,
        )

    def idle(b, r):
        if r % 2:
            return b, r ^ 2
        if r == 0:
            return b ^ 1, r
        return b, r + 2 if r + 2 < bands else 2

    def gather(offsets):
        to = []
        for b in range(groups):
            for r in range(bands):
                offset = offsets[r % 2]
                other = idle(b, r) if offset is None else (b ^ offset, r)
                to.append((b * bands + r, other[0] * bands + other[1]))
        return lax.ppermute(packed, ("blk", "band"), to)

    span = groups // 2
    sources = [packed] + [gather((j, j)) for j in range(1, span)]
    odd_steps = [*range(span, groups)] + [None] * LAG
    even_steps = [*range(span, groups - 1)] + [None] * LAG + [groups - 1]
    rest = [gather(offsets) for offsets in zip(even_steps, odd_steps)]
    hi, lo, own_far = pl.pallas_call(
        functools.partial(left_kernel, width),
        out_shape=[jax.ShapeDtypeStruct((groups, height, deep), jnp.bfloat16)] * 2
        + [jax.ShapeDtypeStruct((width, 2 * pair), f32)],
        in_specs=[vmem()] * 5,
        out_specs=[vmem()] * 3,
        cost_estimate=pl.CostEstimate(
            flops=6 * groups * height * deep * deep, bytes_accessed=2000000, transcendentals=0
        ),
        compiler_params=PARAMS,
        name="left",
    )(source_group, source_row, prolong_code, fine_blocks, packed)

    def products(name, turn, sources, earlier):
        kernel = functools.partial(product_kernel, width, span, turn)
        specs = [pl.BlockSpec(memory_space=pl.ANY)] + [vmem()] * (2 + len(sources))
        shape = (len(sources), height, 2 * pair)
        return call(kernel, name, shape, in_specs=specs)(earlier, hi, lo, *sources)

    parts = [(width, SHIFTS * span * width)] * 3

    def far_part(name, turn, found, last):
        kernel = functools.partial(far_kernel, width, turn)
        return call(kernel, name, parts[0], inputs=4)(hi, lo, found, last)

    far_near = call(functools.partial(near_kernel, width), "near", parts[0], inputs=2 + span)(
        hi, lo, own_far, *sources[1:]
    )
    far = lax.ppermute(far_near, "band", [(i, (i + 1 if i % 2 else i - 1) % bands) for i in range(bands)])
    odd_found = products("rest_odd", 1, rest[: span - 1], far_near)
    far_up = far_part("far_odd", 1, odd_found, rest[span - 1])
    up = lax.ppermute(far_up, "band", [(i, (i + 1) % bands) for i in range(bands)])
    even_found = products("rest_even", 0, rest[: span - 1], far_up)
    far_down = far_part("far_even", 0, even_found, rest[-1])
    down = lax.ppermute(far_down, "band", [((i + 1) % bands, i) for i in range(bands)])
    own_near, own, chip = call(
        functools.partial(join_kernel, width),
        "join",
        [parts[0], parts[0], (2 * width, parts[0][1])],
        in_specs=[pl.BlockSpec(memory_space=pl.ANY)] + [vmem()] * (6 + span),
    )(far_down, hi, lo, odd_found, rest[span - 1], even_found, rest[-1], *sources)
    chip = lax.ppermute(chip, "band", [(i, i ^ 1) for i in range(bands)])
    whole = (width, 5 * groups * width)
    slow = pl.CostEstimate(flops=4000000000, bytes_accessed=2000000, transcendentals=0)
    first = call(functools.partial(first_kernel, groups), "first", whole, inputs=2)(own_near, far)
    early = call(functools.partial(early_kernel, groups), "early", whole, inputs=3, cost_estimate=slow)(
        first, own, up
    )
    return call(functools.partial(late_kernel, groups), "late", whole, inputs=3)(early, down, chip)


def solution(mesh):
    return jax.shard_map(
        body,
        mesh=mesh,
        in_specs=(
            P(("blk", "band"), None, None),
            P(("blk", "band"), None),
            P(("blk", "band"), None),
            P(("blk", "band"), None, None),
            P(("blk", "band"), None),
        ),
        out_specs=P(("blk", "band"), None),
        check_vma=False,
    )
```

```python
import functools

import jax
import jax.numpy as jnp
from jax import lax
from jax.experimental import pallas as pl
from jax.experimental.pallas import tpu as pltpu
from jax.sharding import PartitionSpec as P

SHIFTS = 3
LAG = 1
PARAMS = pltpu.CompilerParams(vmem_limit_bytes=24 * 1024 * 1024)


def vmem():
    return pl.BlockSpec(memory_space=pltpu.VMEM)


def split(x):
    hi = x.astype(jnp.bfloat16)
    return hi, (x - hi.astype(jnp.float32)).astype(jnp.bfloat16)


def dot(a, b):
    return lax.dot_general(a, b, (((1,), (0,)), ((), ())), preferred_element_type=jnp.float32)


def dot3(a_hi, a_lo, b_hi, b_lo):
    return dot(a_hi, b_hi) + (dot(a_hi, b_lo) + dot(a_lo, b_hi))


def lanes_kernel(out_ref):
    pair = out_ref.shape[1]
    out_ref[...] = lax.broadcasted_iota(jnp.int32, out_ref.shape, 1) // (pair // 2)


def pack_kernel(width, lanes_ref, code_ref, p_ref, out_ref):
    deep = p_ref.shape[0]
    rows = deep // width
    out_ref[:deep, :] = p_ref[...]
    left = lanes_ref[...] == 0
    straight = [jnp.where(left, code_ref[0:1, i : i + 1], code_ref[1:2, i : i + 1]) for i in range(rows)]
    crossed = [jnp.where(left, code_ref[1:2, i : i + 1], code_ref[0:1, i : i + 1]) for i in range(rows)]
    out_ref[deep:, :] = jnp.concatenate(straight + crossed, axis=0).astype(jnp.float32)


def left_kernel(width, group_ref, row_ref, code_ref, a_ref, packed_ref, hi_ref, lo_ref, far_ref):
    rows, per_row = group_ref.shape
    groups = hi_ref.shape[0]
    me = lax.axis_index("blk")
    odd = lax.axis_index("band") % 2
    pair = 2 * width
    wide = rows * width
    lane_block = lax.broadcasted_iota(jnp.int32, (rows, wide), 1) // width
    pt = packed_ref[:wide, :].T
    row_of = lane_block[:1]
    codes = []
    for n in range(2):
        c = jnp.broadcast_to(code_ref[n : n + 1, :1], (1, wide))
        for i in range(1, rows):
            c = jnp.where(row_of == i, code_ref[n : n + 1, i : i + 1], c)
        codes.append(c)
    blocks = []
    for dest in (1, 2 - 2 * odd, 2 * odd):
        blocks.append(
            jnp.where(codes[0] == dest, pt[:width], 0.0) + jnp.where(codes[1] == dest, pt[width:], 0.0)
        )
    rt_hi, rt_lo = split(jnp.concatenate(blocks, axis=0))
    left_half = lax.broadcasted_iota(jnp.int32, (width, pair), 1) < width
    twice = []
    for i in range(rows):
        for k in range(0, per_row, 2):
            x = a_ref[i, :, (k // 2) * pair : (k // 2 + 1) * pair]
            y = pltpu.roll(x, width, 1)
            twice += [jnp.where(left_half, x, y), jnp.where(left_half, y, x)]
    slots = [group_ref[:, k : k + 1] ^ me for k in range(per_row)]
    here = [row_ref[:, k : k + 1] == lane_block for k in range(per_row)]
    for j in range(groups):
        chosen = [jnp.where(here[k] & (slots[k] == j), 1, 0) for k in range(per_row)]
        placed = []
        for i in range(rows):
            x = jnp.zeros((width, wide), jnp.float32)
            for k in range(per_row):
                block = twice[i * per_row + k]
                x = jnp.where(chosen[k][i : i + 1] == 1, jnp.concatenate([block] * (rows // 2), axis=1), x)
            placed.append(x)
        b_hi, b_lo = split(jnp.concatenate(placed, axis=0))
        hi_ref[j], lo_ref[j] = split(dot3(rt_hi, rt_lo, b_hi, b_lo))
    far_ref[...] = multiply(hi_ref, lo_ref, 0, packed_ref, width, slice(2 * width, 3 * width))


def spread(src, rows, width):
    lane = lax.broadcasted_iota(jnp.int32, (1, 2 * width), 1)
    low = jnp.where(lane < width, 0.0, 1.0)
    high = jnp.where(lane < width, 2.0, -1.0)
    base = rows * width
    near, far = [], []
    for s in range(rows):
        x = src[s * width : (s + 1) * width, :]
        y = pltpu.roll(x, width, 1)
        straight = src[base + s : base + s + 1, :]
        crossed = src[base + rows + s : base + rows + s + 1, :]
        near.append(jnp.where(straight == low, x, 0.0) + jnp.where(crossed == low, y, 0.0))
        far.append(jnp.where(straight == high, x, 0.0) + jnp.where(crossed == high, y, 0.0))
    return jnp.concatenate([jnp.concatenate(near, axis=0), jnp.concatenate(far, axis=0)], axis=1)


def multiply(hi_ref, lo_ref, slot, src, width, at=slice(None)):
    rows = hi_ref.shape[2] // width
    return dot3(hi_ref[slot, at, :], lo_ref[slot, at, :], *split(spread(src, rows, width)))


def lay_out(found, outs, width):
    swap = lax.axis_index("blk") % 2 == 1
    pair = 2 * width
    pairs = len(found) // 2
    right_half = lax.broadcasted_iota(jnp.int32, (width, pair), 1) >= width
    for q in range(pairs):
        for t, out_ref in enumerate(outs):
            a, b = (f[t * width : (t + 1) * width] for f in found[2 * q : 2 * q + 2])
            before = jnp.where(swap, b, a)
            after = jnp.where(swap, a, b)
            for e in range(SHIFTS):
                tile = slice((e // 2) * pair, (e // 2 + 1) * pair)
                u, v = before[:, tile], after[:, tile]
                if e % 2 == 0:
                    v = pltpu.roll(v, width, 1)
                else:
                    u = pltpu.roll(u, width, 1)
                at = (e * pairs + q) * pair
                out_ref[:, at : at + pair] = jnp.where(right_half, v, u)


def near_kernel(width, hi_ref, lo_ref, own_ref, *refs):
    at = slice(2 * width, 3 * width)
    found = [multiply(hi_ref, lo_ref, 1 + j, src, width, at) for j, src in enumerate(refs[:-1])]
    lay_out([own_ref[...]] + found, refs[-1:], width)


def product_kernel(width, first, turn, earlier_ref, hi_ref, lo_ref, *refs):
    sources, out_ref = refs[:-1], refs[-1]

    @pl.when(lax.axis_index("band") % 2 == turn)
    def _():
        for j, src in enumerate(sources):
            out_ref[j] = multiply(hi_ref, lo_ref, first + j, src, width)


def finish(width, at, hi_ref, lo_ref, found_ref, last_ref, outs):
    found = [found_ref[j, at, :] for j in range(found_ref.shape[0])]
    found.append(multiply(hi_ref, lo_ref, hi_ref.shape[0] - 1, last_ref, width, at))
    lay_out(found, outs, width)


def far_kernel(width, turn, hi_ref, lo_ref, found_ref, last_ref, out_ref):
    mine = lax.axis_index("band") % 2 == turn

    @pl.when(mine)
    def _():
        finish(width, slice(2 * width, 3 * width), hi_ref, lo_ref, found_ref, last_ref, [out_ref])

    @pl.when(jnp.logical_not(mine))
    def _():
        out_ref[...] = jnp.zeros_like(out_ref)


def join_kernel(width, earlier_ref, hi_ref, lo_ref, *refs):
    sources, (near_ref, rest_ref, chip_ref) = refs[4:-3], refs[-3:]
    odd = lax.axis_index("band") % 2 == 1
    at = slice(0, 2 * width)
    found = [multiply(hi_ref, lo_ref, j, src, width, at) for j, src in enumerate(sources)]
    lay_out(found, [near_ref, chip_ref.at[:width]], width)
    outs = [rest_ref, chip_ref.at[width:]]
    pl.when(odd)(lambda: finish(width, at, hi_ref, lo_ref, refs[0], refs[1], outs))
    pl.when(jnp.logical_not(odd))(lambda: finish(width, at, hi_ref, lo_ref, refs[2], refs[3], outs))


def place(sum_ref, part_ref, groups, first, shift):
    me = lax.axis_index("blk")
    pair = 2 * part_ref.shape[0]
    pairs = part_ref.shape[1] // (SHIFTS * pair)
    for q in range(pairs):
        tile = (me ^ (first + 2 * q)) // 2
        for e in range(SHIFTS):
            at = pl.ds(pl.multiple_of(((e + shift) * (groups // 2) + tile) * pair, pair), pair)
            sum_ref[:, at] += part_ref[:, (e * pairs + q) * pair : (e * pairs + q + 1) * pair]


def first_kernel(groups, near_ref, far_ref, out_ref):
    out_ref[...] = jnp.zeros_like(out_ref)
    place(out_ref, near_ref, groups, 0, 1)
    place(out_ref, far_ref, groups, 0, 2 * (lax.axis_index("band") % 2))


def early_kernel(groups, first_ref, rest_ref, up_ref, out_ref):
    span = groups // 2
    out_ref[...] = first_ref[...]
    place(out_ref, rest_ref, groups, span, 1)
    place(out_ref, up_ref, groups, span, 0)


def late_kernel(groups, early_ref, down_ref, chip_ref, out_ref):
    odd = lax.axis_index("band") % 2
    span = groups // 2
    height = early_ref.shape[0]
    out_ref[...] = early_ref[...]
    place(out_ref, chip_ref.at[:height], groups, 0, 2 - 2 * odd)
    place(out_ref, chip_ref.at[height:], groups, span, 2 - 2 * odd)
    place(out_ref, down_ref, groups, span, 2)


def body(fine_blocks, source_group, source_row, prolong_blocks, prolong_code):
    rows, width, pair = prolong_blocks.shape
    groups = lax.axis_size("blk")
    bands = lax.axis_size("band")
    f32 = jnp.float32
    prolong_code = prolong_code.T
    lanes = pl.pallas_call(
        lanes_kernel,
        out_shape=jax.ShapeDtypeStruct((1, pair), jnp.int32),
        out_specs=vmem(),
        cost_estimate=pl.CostEstimate(flops=4000000000, bytes_accessed=10000000, transcendentals=0),
        compiler_params=PARAMS,
        name="lanes",
    )()
    packed = pl.pallas_call(
        functools.partial(pack_kernel, width),
        out_shape=jax.ShapeDtypeStruct((rows * width + 2 * rows, pair), f32),
        in_specs=[vmem()] * 3,
        out_specs=vmem(),
        compiler_params=PARAMS,
        name="pack",
    )(lanes, prolong_code, prolong_blocks.reshape(rows * width, pair))
    height = SHIFTS * width
    deep = rows * width

    def call(kernel, name, shapes, dtype=f32, inputs=0, **more):
        more.setdefault("in_specs", [vmem()] * inputs)
        single = not isinstance(shapes, list)
        out = [jax.ShapeDtypeStruct(x, dtype) for x in ([shapes] if single else shapes)]
        return pl.pallas_call(
            kernel,
            out_shape=out[0] if single else out,
            out_specs=vmem() if single else [vmem()] * len(out),
            compiler_params=PARAMS,
            name=name,
            **more,
        )

    def idle(b, r):
        if r % 2:
            return b, r ^ 2
        if r in (0, 2):
            return b ^ 1, r
        return b, r + 2 if r % 4 == 0 else r - 2

    def gather(offsets):
        to = []
        for b in range(groups):
            for r in range(bands):
                offset = offsets[r % 2]
                other = idle(b, r) if offset is None else (b ^ offset, r)
                to.append((b * bands + r, other[0] * bands + other[1]))
        return lax.ppermute(packed, ("blk", "band"), to)

    span = groups // 2
    sources = [packed] + [gather((j, j)) for j in range(1, span)]
    odd_steps = [*range(span, groups)] + [None] * LAG
    even_steps = [*range(span, groups - 1)] + [None] * LAG + [groups - 1]
    rest = [gather(offsets) for offsets in zip(even_steps, odd_steps)]
    hi, lo, own_far = pl.pallas_call(
        functools.partial(left_kernel, width),
        out_shape=[jax.ShapeDtypeStruct((groups, height, deep), jnp.bfloat16)] * 2
        + [jax.ShapeDtypeStruct((width, 2 * pair), f32)],
        in_specs=[vmem()] * 5,
        out_specs=[vmem()] * 3,
        cost_estimate=pl.CostEstimate(
            flops=6 * groups * height * deep * deep, bytes_accessed=2000000, transcendentals=0
        ),
        compiler_params=PARAMS,
        name="left",
    )(source_group, source_row, prolong_code, fine_blocks, packed)

    def products(name, turn, sources, earlier):
        kernel = functools.partial(product_kernel, width, span, turn)
        specs = [pl.BlockSpec(memory_space=pl.ANY)] + [vmem()] * (2 + len(sources))
        shape = (len(sources), height, 2 * pair)
        return call(kernel, name, shape, in_specs=specs)(earlier, hi, lo, *sources)

    parts = [(width, SHIFTS * span * width)] * 3

    def far_part(name, turn, found, last):
        kernel = functools.partial(far_kernel, width, turn)
        return call(kernel, name, parts[0], inputs=4)(hi, lo, found, last)

    far_near = call(functools.partial(near_kernel, width), "near", parts[0], inputs=2 + span)(
        hi, lo, own_far, *sources[1:]
    )
    far = lax.ppermute(far_near, "band", [(i, (i + 1 if i % 2 else i - 1) % bands) for i in range(bands)])
    odd_found = products("rest_odd", 1, rest[: span - 1], far_near)
    far_up = far_part("far_odd", 1, odd_found, rest[span - 1])
    up = lax.ppermute(far_up, "band", [(i, (i + 1) % bands) for i in range(bands)])
    even_found = products("rest_even", 0, rest[: span - 1], far_up)
    far_down = far_part("far_even", 0, even_found, rest[-1])
    down = lax.ppermute(far_down, "band", [((i + 1) % bands, i) for i in range(bands)])
    own_near, own, chip = call(
        functools.partial(join_kernel, width),
        "join",
        [parts[0], parts[0], (2 * width, parts[0][1])],
        in_specs=[pl.BlockSpec(memory_space=pl.ANY)] + [vmem()] * (6 + span),
    )(far_down, hi, lo, odd_found, rest[span - 1], even_found, rest[-1], *sources)
    chip = lax.ppermute(chip, "band", [(i, i ^ 1) for i in range(bands)])
    whole = (width, 5 * groups * width)
    slow = pl.CostEstimate(flops=4000000000, bytes_accessed=2000000, transcendentals=0)
    first = call(functools.partial(first_kernel, groups), "first", whole, inputs=2)(own_near, far)
    early = call(functools.partial(early_kernel, groups), "early", whole, inputs=3, cost_estimate=slow)(
        first, own, up
    )
    return call(functools.partial(late_kernel, groups), "late", whole, inputs=3)(early, down, chip)


def solution(mesh):
    return jax.shard_map(
        body,
        mesh=mesh,
        in_specs=(
            P(("blk", "band"), None, None),
            P(("blk", "band"), None),
            P(("blk", "band"), None),
            P(("blk", "band"), None, None),
            P(("blk", "band"), None),
        ),
        out_specs=P(("blk", "band"), None),
        check_vma=False,
    )
```

```python
import functools

import jax
import jax.numpy as jnp
from jax import lax
from jax.experimental import pallas as pl
from jax.experimental.pallas import tpu as pltpu
from jax.sharding import PartitionSpec as P

SHIFTS = 3
LAG = 1
PARAMS = pltpu.CompilerParams(vmem_limit_bytes=24 * 1024 * 1024)


def vmem():
    return pl.BlockSpec(memory_space=pltpu.VMEM)


def split(x):
    hi = x.astype(jnp.bfloat16)
    return hi, (x - hi.astype(jnp.float32)).astype(jnp.bfloat16)


def dot(a, b):
    return lax.dot_general(a, b, (((1,), (0,)), ((), ())), preferred_element_type=jnp.float32)


def dot3(a_hi, a_lo, b_hi, b_lo):
    height = a_hi.shape[0]
    both = dot(jnp.concatenate([a_hi, a_lo], axis=0), b_hi)
    return both[:height] + (dot(a_hi, b_lo) + both[height:])


def lanes_kernel(out_ref):
    pair = out_ref.shape[1]
    out_ref[...] = lax.broadcasted_iota(jnp.int32, out_ref.shape, 1) // (pair // 2)


def pack_kernel(width, lanes_ref, code_ref, p_ref, out_ref):
    deep = p_ref.shape[0]
    rows = deep // width
    out_ref[:deep, :] = p_ref[...]
    left = lanes_ref[...] == 0
    straight = [jnp.where(left, code_ref[0:1, i : i + 1], code_ref[1:2, i : i + 1]) for i in range(rows)]
    crossed = [jnp.where(left, code_ref[1:2, i : i + 1], code_ref[0:1, i : i + 1]) for i in range(rows)]
    out_ref[deep:, :] = jnp.concatenate(straight + crossed, axis=0).astype(jnp.float32)


def left_kernel(width, group_ref, row_ref, code_ref, a_ref, packed_ref, hi_ref, lo_ref, far_ref):
    rows, per_row = group_ref.shape
    groups = hi_ref.shape[0]
    me = lax.axis_index("blk")
    odd = lax.axis_index("band") % 2
    pair = 2 * width
    wide = rows * width
    lane_block = lax.broadcasted_iota(jnp.int32, (rows, wide), 1) // width
    pt = packed_ref[:wide, :].T
    row_of = lane_block[:1]
    codes = []
    for n in range(2):
        c = jnp.broadcast_to(code_ref[n : n + 1, :1], (1, wide))
        for i in range(1, rows):
            c = jnp.where(row_of == i, code_ref[n : n + 1, i : i + 1], c)
        codes.append(c)
    blocks = []
    for dest in (1, 2 - 2 * odd, 2 * odd):
        blocks.append(
            jnp.where(codes[0] == dest, pt[:width], 0.0) + jnp.where(codes[1] == dest, pt[width:], 0.0)
        )
    rt_hi, rt_lo = split(jnp.concatenate(blocks, axis=0))
    left_half = lax.broadcasted_iota(jnp.int32, (width, pair), 1) < width
    twice = []
    for i in range(rows):
        for k in range(0, per_row, 2):
            x = a_ref[i, :, (k // 2) * pair : (k // 2 + 1) * pair]
            y = pltpu.roll(x, width, 1)
            twice += [jnp.where(left_half, x, y), jnp.where(left_half, y, x)]
    slots = [group_ref[:, k : k + 1] ^ me for k in range(per_row)]
    here = [row_ref[:, k : k + 1] == lane_block for k in range(per_row)]
    for j in range(groups):
        chosen = [jnp.where(here[k] & (slots[k] == j), 1, 0) for k in range(per_row)]
        placed = []
        for i in range(rows):
            x = jnp.zeros((width, wide), jnp.float32)
            for k in range(per_row):
                block = twice[i * per_row + k]
                x = jnp.where(chosen[k][i : i + 1] == 1, jnp.concatenate([block] * (rows // 2), axis=1), x)
            placed.append(x)
        b_hi, b_lo = split(jnp.concatenate(placed, axis=0))
        hi_ref[j], lo_ref[j] = split(dot3(rt_hi, rt_lo, b_hi, b_lo))
    far_ref[...] = multiply(hi_ref, lo_ref, 0, packed_ref, width, slice(2 * width, 3 * width))


def spread(src, rows, width):
    lane = lax.broadcasted_iota(jnp.int32, (1, 2 * width), 1)
    low = jnp.where(lane < width, 0.0, 1.0)
    high = jnp.where(lane < width, 2.0, -1.0)
    base = rows * width
    near, far = [], []
    for s in range(rows):
        x = src[s * width : (s + 1) * width, :]
        y = pltpu.roll(x, width, 1)
        straight = src[base + s : base + s + 1, :]
        crossed = src[base + rows + s : base + rows + s + 1, :]
        near.append(jnp.where(straight == low, x, 0.0) + jnp.where(crossed == low, y, 0.0))
        far.append(jnp.where(straight == high, x, 0.0) + jnp.where(crossed == high, y, 0.0))
    return jnp.concatenate([jnp.concatenate(near, axis=0), jnp.concatenate(far, axis=0)], axis=1)


def multiply(hi_ref, lo_ref, slot, src, width, at=slice(None)):
    rows = hi_ref.shape[2] // width
    return dot3(hi_ref[slot, at, :], lo_ref[slot, at, :], *split(spread(src, rows, width)))


def lay_out(found, outs, width):
    swap = lax.axis_index("blk") % 2 == 1
    pair = 2 * width
    pairs = len(found) // 2
    right_half = lax.broadcasted_iota(jnp.int32, (width, pair), 1) >= width
    for q in range(pairs):
        for t, out_ref in enumerate(outs):
            a, b = (f[t * width : (t + 1) * width] for f in found[2 * q : 2 * q + 2])
            before = jnp.where(swap, b, a)
            after = jnp.where(swap, a, b)
            for e in range(SHIFTS):
                tile = slice((e // 2) * pair, (e // 2 + 1) * pair)
                u, v = before[:, tile], after[:, tile]
                if e % 2 == 0:
                    v = pltpu.roll(v, width, 1)
                else:
                    u = pltpu.roll(u, width, 1)
                at = (e * pairs + q) * pair
                out_ref[:, at : at + pair] = jnp.where(right_half, v, u)


def near_kernel(width, hi_ref, lo_ref, own_ref, *refs):
    at = slice(2 * width, 3 * width)
    found = [multiply(hi_ref, lo_ref, 1 + j, src, width, at) for j, src in enumerate(refs[:-1])]
    lay_out([own_ref[...]] + found, refs[-1:], width)


def product_kernel(width, first, turn, earlier_ref, hi_ref, lo_ref, *refs):
    sources, out_ref = refs[:-1], refs[-1]

    @pl.when(lax.axis_index("band") % 2 == turn)
    def _():
        for j, src in enumerate(sources):
            out_ref[j] = multiply(hi_ref, lo_ref, first + j, src, width)


def finish(width, at, hi_ref, lo_ref, found_ref, last_ref, outs):
    found = [found_ref[j, at, :] for j in range(found_ref.shape[0])]
    found.append(multiply(hi_ref, lo_ref, hi_ref.shape[0] - 1, last_ref, width, at))
    lay_out(found, outs, width)


def far_kernel(width, turn, hi_ref, lo_ref, found_ref, last_ref, out_ref):
    mine = lax.axis_index("band") % 2 == turn

    @pl.when(mine)
    def _():
        finish(width, slice(2 * width, 3 * width), hi_ref, lo_ref, found_ref, last_ref, [out_ref])

    @pl.when(jnp.logical_not(mine))
    def _():
        out_ref[...] = jnp.zeros_like(out_ref)


def join_kernel(width, earlier_ref, hi_ref, lo_ref, *refs):
    sources, (near_ref, rest_ref, chip_ref) = refs[4:-3], refs[-3:]
    odd = lax.axis_index("band") % 2 == 1
    at = slice(0, 2 * width)
    found = [multiply(hi_ref, lo_ref, j, src, width, at) for j, src in enumerate(sources)]
    lay_out(found, [near_ref, chip_ref.at[:width]], width)
    outs = [rest_ref, chip_ref.at[width:]]
    pl.when(odd)(lambda: finish(width, at, hi_ref, lo_ref, refs[0], refs[1], outs))
    pl.when(jnp.logical_not(odd))(lambda: finish(width, at, hi_ref, lo_ref, refs[2], refs[3], outs))


def place(sum_ref, part_ref, groups, first, shift):
    me = lax.axis_index("blk")
    pair = 2 * part_ref.shape[0]
    pairs = part_ref.shape[1] // (SHIFTS * pair)
    for q in range(pairs):
        tile = (me ^ (first + 2 * q)) // 2
        for e in range(SHIFTS):
            at = pl.ds(pl.multiple_of(((e + shift) * (groups // 2) + tile) * pair, pair), pair)
            sum_ref[:, at] += part_ref[:, (e * pairs + q) * pair : (e * pairs + q + 1) * pair]


def first_kernel(groups, near_ref, far_ref, out_ref):
    out_ref[...] = jnp.zeros_like(out_ref)
    place(out_ref, near_ref, groups, 0, 1)
    place(out_ref, far_ref, groups, 0, 2 * (lax.axis_index("band") % 2))


def early_kernel(groups, first_ref, rest_ref, up_ref, out_ref):
    span = groups // 2
    out_ref[...] = first_ref[...]
    place(out_ref, rest_ref, groups, span, 1)
    place(out_ref, up_ref, groups, span, 0)


def late_kernel(groups, early_ref, down_ref, chip_ref, out_ref):
    odd = lax.axis_index("band") % 2
    span = groups // 2
    height = early_ref.shape[0]
    out_ref[...] = early_ref[...]
    place(out_ref, chip_ref.at[:height], groups, 0, 2 - 2 * odd)
    place(out_ref, chip_ref.at[height:], groups, span, 2 - 2 * odd)
    place(out_ref, down_ref, groups, span, 2)


def body(fine_blocks, source_group, source_row, prolong_blocks, prolong_code):
    rows, width, pair = prolong_blocks.shape
    groups = lax.axis_size("blk")
    bands = lax.axis_size("band")
    f32 = jnp.float32
    prolong_code = prolong_code.T
    lanes = pl.pallas_call(
        lanes_kernel,
        out_shape=jax.ShapeDtypeStruct((1, pair), jnp.int32),
        out_specs=vmem(),
        cost_estimate=pl.CostEstimate(flops=4000000000, bytes_accessed=10000000, transcendentals=0),
        compiler_params=PARAMS,
        name="lanes",
    )()
    packed = pl.pallas_call(
        functools.partial(pack_kernel, width),
        out_shape=jax.ShapeDtypeStruct((rows * width + 2 * rows, pair), f32),
        in_specs=[vmem()] * 3,
        out_specs=vmem(),
        compiler_params=PARAMS,
        name="pack",
    )(lanes, prolong_code, prolong_blocks.reshape(rows * width, pair))
    height = SHIFTS * width
    deep = rows * width

    def call(kernel, name, shapes, dtype=f32, inputs=0, **more):
        more.setdefault("in_specs", [vmem()] * inputs)
        single = not isinstance(shapes, list)
        out = [jax.ShapeDtypeStruct(x, dtype) for x in ([shapes] if single else shapes)]
        return pl.pallas_call(
            kernel,
            out_shape=out[0] if single else out,
            out_specs=vmem() if single else [vmem()] * len(out),
            compiler_params=PARAMS,
            name=name,
            **more,
        )

    def idle(b, r):
        if r % 2:
            return b, r ^ 2
        if r == 0:
            return b ^ 1, r
        return b, r + 2 if r + 2 < bands else 2

    def gather(offsets):
        to = []
        for b in range(groups):
            for r in range(bands):
                offset = offsets[r % 2]
                other = idle(b, r) if offset is None else (b ^ offset, r)
                to.append((b * bands + r, other[0] * bands + other[1]))
        return lax.ppermute(packed, ("blk", "band"), to)

    span = groups // 2
    sources = [packed] + [gather((j, j)) for j in range(1, span)]
    odd_steps = [*range(span, groups)] + [None] * LAG
    even_steps = [*range(span, groups - 1)] + [None] * LAG + [groups - 1]
    rest = [gather(offsets) for offsets in zip(even_steps, odd_steps)]
    hi, lo, own_far = pl.pallas_call(
        functools.partial(left_kernel, width),
        out_shape=[jax.ShapeDtypeStruct((groups, height, deep), jnp.bfloat16)] * 2
        + [jax.ShapeDtypeStruct((width, 2 * pair), f32)],
        in_specs=[vmem()] * 5,
        out_specs=[vmem()] * 3,
        cost_estimate=pl.CostEstimate(
            flops=6 * groups * height * deep * deep, bytes_accessed=2000000, transcendentals=0
        ),
        compiler_params=PARAMS,
        name="left",
    )(source_group, source_row, prolong_code, fine_blocks, packed)

    def products(name, turn, sources, earlier):
        kernel = functools.partial(product_kernel, width, span, turn)
        specs = [pl.BlockSpec(memory_space=pl.ANY)] + [vmem()] * (2 + len(sources))
        shape = (len(sources), height, 2 * pair)
        return call(kernel, name, shape, in_specs=specs)(earlier, hi, lo, *sources)

    parts = [(width, SHIFTS * span * width)] * 3

    def far_part(name, turn, found, last):
        kernel = functools.partial(far_kernel, width, turn)
        return call(kernel, name, parts[0], inputs=4)(hi, lo, found, last)

    far_near = call(functools.partial(near_kernel, width), "near", parts[0], inputs=2 + span)(
        hi, lo, own_far, *sources[1:]
    )
    far = lax.ppermute(far_near, "band", [(i, (i + 1 if i % 2 else i - 1) % bands) for i in range(bands)])
    odd_found = products("rest_odd", 1, rest[: span - 1], far_near)
    far_up = far_part("far_odd", 1, odd_found, rest[span - 1])
    up = lax.ppermute(far_up, "band", [(i, (i + 1) % bands) for i in range(bands)])
    even_found = products("rest_even", 0, rest[: span - 1], far_up)
    far_down = far_part("far_even", 0, even_found, rest[-1])
    down = lax.ppermute(far_down, "band", [((i + 1) % bands, i) for i in range(bands)])
    own_near, own, chip = call(
        functools.partial(join_kernel, width),
        "join",
        [parts[0], parts[0], (2 * width, parts[0][1])],
        in_specs=[pl.BlockSpec(memory_space=pl.ANY)] + [vmem()] * (6 + span),
    )(far_down, hi, lo, odd_found, rest[span - 1], even_found, rest[-1], *sources)
    chip = lax.ppermute(chip, "band", [(i, i ^ 1) for i in range(bands)])
    whole = (width, 5 * groups * width)
    slow = pl.CostEstimate(flops=4000000000, bytes_accessed=2000000, transcendentals=0)
    first = call(functools.partial(first_kernel, groups), "first", whole, inputs=2)(own_near, far)
    early = call(functools.partial(early_kernel, groups), "early", whole, inputs=3, cost_estimate=slow)(
        first, own, up
    )
    return call(functools.partial(late_kernel, groups), "late", whole, inputs=3)(early, down, chip)


def solution(mesh):
    return jax.shard_map(
        body,
        mesh=mesh,
        in_specs=(
            P(("blk", "band"), None, None),
            P(("blk", "band"), None),
            P(("blk", "band"), None),
            P(("blk", "band"), None, None),
            P(("blk", "band"), None),
        ),
        out_specs=P(("blk", "band"), None),
        check_vma=False,
    )
```
